128 devices in a mesh: rep: 8 (over z, y_hi), shard: 16 (over y_lo, x, core).
Axes of the slice: x: 4, y: 4 (y_hi: 2, y_lo: 2; y = y_hi * 2 + y_lo), z: 4, core: 2. Of those that a mesh axis runs over, the one named last changes fastest.
Arguments:
- tokens: bfloat16 [65536, 4096], P(('rep', 'shard')), may hold values from -24 to 24
- hidden_grad: bfloat16 [65536, 896], P(('rep', 'shard')), may hold values from -6 to 6
- master: float32 [4096, 1792], P('shard'), may hold values from -6 to 6
- moment_first: float32 [4096, 1792], P('shard'), may hold values from -6 to 6
- moment_second: float32 [4096, 1792], P('shard'), may hold values from 0.5 to 8
Outputs:
- input_grad: bfloat16 [65536, 4096], P(('rep', 'shard'))
- master_next: float32 [4096, 1792], P('shard')
- first_next: float32 [4096, 1792], P('shard')
- second_next: float32 [4096, 1792], P('shard')
The draws below stay inside these ranges and needn't reach their ends.
All inputs are finite; a program needn't handle non-finite values.
Results may differ from the reference program's by a relative error of at most 0.029.
Values may be sent and summed in bfloat16 or wider, within the bound.
A program may use at most 128 MiB of HBM per device.

```python
import math
import jax
import jax.numpy as jnp
from jax import lax

D = 4096
FFW = 896
TOK_DEV = 512
TOKENS = 65536


def raised(drawn, rng, source, target, parts, factor):
    owner, partner = [(jnp.arange(drawn.shape[dim]) // (drawn.shape[dim] // parts)).reshape([-1 if axis == dim else 1 for axis in range(drawn.ndim)]) for dim in (source, target)]
    chosen = jax.random.permutation(rng, parts)[partner]
    strong = (owner == chosen) | (owner == (partner + parts // 2) % parts)
    return jnp.where(strong, factor * drawn, drawn)


def block_levels(key, dims, shards, least, high):
    loudness, own = 1.0, jax.random.fold_in(key, 6)
    for dim, parts in shards:
        draws = jnp.exp(jax.random.uniform(jax.random.fold_in(own, dim), (parts,), jnp.float32, least / len(shards), high / len(shards)))
        loudness = loudness * jnp.repeat(draws, dims[dim] // parts).reshape([-1 if axis == dim else 1 for axis in range(len(dims))])
    return loudness


def gaussian(own_key, dims, spread, most, shards=(), kind=jnp.bfloat16):
    values = spread * jax.random.normal(own_key, dims, jnp.float32)
    if shards:
        values = values * block_levels(own_key, dims, shards, -0.22, 0.18)
    return jnp.clip(values, -most, most).astype(kind)


def bell_draw_with(key, extent, scale, limit, split, heavy, held_as=jnp.bfloat16):
    entries = scale * jax.random.normal(key, extent, jnp.float32)
    if split:
        entries = entries * block_levels(key, extent, split, -0.22, 0.18)
    return jnp.clip(raised(entries, jax.random.fold_in(key, 3), *heavy), -limit, limit).astype(held_as)


def setup_inputs(seed: int = 0) -> dict:
    arg_keys = jax.random.split(jax.random.key(seed), 6)
    return {
        "tokens": bell_draw_with(arg_keys[0], (TOKENS, D), 1.0, 24.0, ((0, 128),), (0, 1, 128, 5.5)),
        "hidden_grad": gaussian(arg_keys[1], (TOKENS, FFW), 1.0, 6.0, ((0, 128),)),
        "master": gaussian(arg_keys[2], (D, 2 * FFW), 1.0, 6.0, ((0, 16),), jnp.float32),
        "moment_first": gaussian(arg_keys[3], (D, 2 * FFW), 1.0, 6.0, ((0, 16),), jnp.float32),
        "moment_second": jnp.clip(jnp.exp(math.log(8.0) - 2.7725887 * jax.random.uniform(arg_keys[4], (D, 2 * FFW), jnp.float32) ** block_levels(arg_keys[4], (D, 2 * FFW), ((0, 16),), -0.2, 0.2)), 0.5, 8.0),
    }


bias_first = 0.999973438601
bias_second = 0.99407947078

def adamw(master, moment_first, moment_second, grad):
    first_next = 0.9 * moment_first + 0.1 * grad
    second_next = 0.95 * moment_second + 0.05 * grad * grad
    corrected_one = first_next / bias_first
    corrected_two = second_next / bias_second
    update = corrected_one / (jnp.sqrt(corrected_two) + 1e-08) + 0.1 * master
    return (master - 0.01 * update, first_next, second_next)

def reference(tokens, hidden_grad, master, moment_first, moment_second):
    multiplier = D ** (-0.5)
    weights = master.astype(jnp.bfloat16)

    def device_block(running, position):
        first_row = (position * TOK_DEV).astype(jnp.int32)
        token_rows = lax.dynamic_slice_in_dim(tokens, first_row, TOK_DEV, 0)
        cotangent_rows = lax.dynamic_slice_in_dim(hidden_grad, first_row, TOK_DEV, 0).astype(jnp.float32)
        gate_up = jnp.dot(token_rows, weights, preferred_element_type=jnp.float32) * multiplier
        gate = gate_up[:, :FFW]
        upward = gate_up[:, FFW:]
        sigmoid_gate = jax.nn.sigmoid(gate)
        grad_gate = cotangent_rows * upward * sigmoid_gate * (1.0 + gate * (1.0 - sigmoid_gate))
        grad_up = cotangent_rows * gate * sigmoid_gate
        branch_grad = jnp.concatenate([grad_gate, grad_up], axis=1).astype(jnp.bfloat16)
        input_rows = lax.dot_general(branch_grad, weights, (((1,), (1,)), ((), ())), preferred_element_type=jnp.float32)
        input_rows = (input_rows * multiplier).astype(jnp.bfloat16)
        partial_value = lax.dot_general(token_rows, branch_grad, (((0,), (0,)), ((), ())), preferred_element_type=jnp.float32)
        partial_value = (partial_value * multiplier).astype(jnp.bfloat16)
        return (running + partial_value.astype(jnp.float32), input_rows)
    blocks = TOKENS // TOK_DEV
    start_grad = jnp.zeros((D, 2 * FFW), jnp.float32)
    grad, input_blocks = lax.scan(device_block, start_grad, jnp.arange(blocks, dtype=jnp.int32))
    input_grad = input_blocks.reshape(TOKENS, D)
    master_next, first_next, second_next = adamw(master, moment_first, moment_second, grad)
    return (input_grad, master_next, first_next, second_next)
```

```python
import jax
import jax.numpy as jnp
from jax import lax
from jax.experimental import pallas as pl
from jax.experimental.pallas import tpu as pltpu
from jax.sharding import PartitionSpec as P

MESH = pl.DeviceIdType.MESH
bias_first = 0.999973438601
bias_second = 0.99407947078
bf16, f32 = jnp.bfloat16, jnp.float32

D, FFW, TOK = 4096, 896, 512
UNIT = 512
HALF = 256
WIDTHS = (256, 256, 256, 128)
NCHUNK = len(WIDTHS)
MULT = 1.0 / 64.0
N_SEM = 160


def adamw(master, moment_first, moment_second, grad):
    first_next = 0.9 * moment_first + 0.1 * grad
    second_next = 0.95 * moment_second + 0.05 * grad * grad
    corrected_one = first_next / bias_first
    corrected_two = second_next / bias_second
    update = corrected_one / (jnp.sqrt(corrected_two) + 1e-08) + 0.1 * master
    return (master - 0.01 * update, first_next, second_next)


def add(*values):
    total = values[0].astype(f32)
    for v in values[1:]:
        total = total + v.astype(f32)
    return total


def kernel(
    tokens, hidden, master, ig_out, g_out,
    tok, tok_t, hid, mst, branch, ig_in,
    w_a, w_h, snd_a, snd_h, g_a, g_h, yr_a, yr_h, x1_a, x1_h, x2_a, x2_h,
    zr_a, zr_h, yh_a, yh_h, fin_a, fin_h, sw_a, sw_h,
    lsem, ssem, rsem,
):
    rep, shard = lax.axis_index("rep"), lax.axis_index("shard")
    z, y_hi = rep // 2, rep % 2
    y_lo, x, c = shard // 8, (shard // 2) % 4, shard % 2
    y = y_hi * 2 + y_lo
    mine = y_lo * 4 + x

    def device(dx=0, dy=0, dz=0, dc=0):
        xx, yy, zz, cc = (x + dx + 4) % 4, (y + dy + 4) % 4, (z + dz + 4) % 4, (c + dc) % 2
        return (zz * 2 + yy // 2, ((yy % 2) * 4 + xx) * 2 + cc)

    sibling = device(dc=1)
    right, left = device(dx=1), device(dx=-1)
    up, down = device(dy=1), device(dy=-1)
    far_y = device(dy=2)
    z_next = [device(dz=1), device(dz=-1), device(dz=2)]
    partners = [sibling, right, left, up, down, far_y] + z_next

    def split(a, h):
        return [a.at[0], a.at[1], a.at[2], h]

    w, snd, g = split(w_a, w_h), split(snd_a, snd_h), split(g_a, g_h)
    yr, x1, x2 = split(yr_a, yr_h), split(x1_a, x1_h), split(x2_a, x2_h)
    zr, yh, fin, sw = split(zr_a, zr_h), split(yh_a, yh_h), split(fin_a, fin_h), split(sw_a, sw_h)

    sent = []

    def send(src, dst, to):
        i = len(sent)
        copy = pltpu.make_async_remote_copy(
            src_ref=src, dst_ref=dst, send_sem=ssem.at[i], recv_sem=rsem.at[i],
            device_id=to, device_id_type=MESH,
        )
        copy.start()
        sent.append(copy)
        return copy

    local = []

    def fetch(src, dst):
        copy = pltpu.make_async_copy(src, dst, lsem.at[len(local)])
        copy.start()
        local.append(copy)
        return copy

    def hidden_cols(core):
        return pl.ds(pl.multiple_of(core * 384, 128), 512)

    got_master = fetch(master, mst)
    got_tok = fetch(tokens, tok.at[pl.ds(0, TOK)])
    got_hid = fetch(hidden.at[:, hidden_cols(c)], hid.at[pl.ds(0, TOK)])

    barrier = pltpu.get_barrier_semaphore()
    for p in partners:
        pl.semaphore_signal(barrier, inc=1, device_id=p, device_id_type=MESH)
    pl.semaphore_wait(barrier, len(partners))

    my_rows = pl.ds(pl.multiple_of(c * HALF, HALF), HALF)
    other_rows = pl.ds(pl.multiple_of((1 - c) * HALF, HALF), HALF)

    def cols(core, k, part):
        return pl.ds(pl.multiple_of(part * FFW + (core * 4 + k) * 128, 128), 128)

    low = lax.broadcasted_iota(jnp.int32, (HALF, 128), 1) < 64
    got_master.wait()
    swapped = []
    for k in range(NCHUNK):
        if k < 3:
            for part in range(2):
                there = pl.ds(part * 128, 128)
                snd[k][:, there] = mst[:, cols(1 - c, k, part)].astype(bf16)
                w[k][mine, my_rows, there] = mst[:, cols(c, k, part)].astype(bf16)
        else:
            gate, upw = mst[:, 384:512], pltpu.roll(mst[:, FFW + 384 : FFW + 512], 64, 1)
            own_first = jnp.logical_xor(low, jnp.broadcast_to(c == 1, low.shape))
            w[k][mine, my_rows, :] = jnp.where(own_first, gate, upw).astype(bf16)
            snd[k][...] = jnp.where(own_first, upw, gate).astype(bf16)
        swapped.append(send(snd[k], w[k].at[mine, my_rows], sibling))
    tok_in = send(tokens, tok.at[pl.ds(TOK, TOK)], sibling)
    hid_in = send(hidden.at[:, hidden_cols(1 - c)], hid.at[pl.ds(TOK, TOK)], sibling)

    A, B, ALL = pl.ds(0, 256), pl.ds(256, 256), pl.ds(0, 512)
    gat = [{} for _ in range(NCHUNK)]

    def unit_x(dx):
        return y_lo * 4 + (x + dx + 4) % 4

    def relay(k, unit, rows, to):
        part = w[k].at[unit, rows]
        return send(part, part, to)

    def to_y(k, name, unit):
        gat[k][name] = (relay(k, unit, A, up), relay(k, unit, B, down))

    def ag_start(k):
        swapped[k].wait_recv()
        gat[k]["right"] = relay(k, mine, ALL, right)
        gat[k]["left"] = relay(k, mine, ALL, left)
        to_y(k, "y0", mine)

    def ag_relay(k):
        gat[k]["right"].wait_recv()
        gat[k]["p"] = relay(k, unit_x(-1), A, right)
        gat[k]["left"].wait_recv()
        gat[k]["q"] = relay(k, unit_x(1), B, left)
        to_y(k, "y1", unit_x(-1))
        to_y(k, "y2", unit_x(1))

    def ag_relay2(k):
        gat[k]["p"].wait_recv()
        gat[k]["q"].wait_recv()
        to_y(k, "y3", unit_x(2))

    def ag_done(k):
        for name in ("y0", "y1", "y2", "y3"):
            for copy in gat[k][name]:
                copy.wait_recv()

    def transpose(half):
        @pl.loop(0, 8)
        def _(i):
            cut = pl.ds(pl.multiple_of(i * 512, 512), 512)
            tok_t[cut, pl.ds(half * TOK, TOK)] = tok[pl.ds(half * TOK, TOK), cut].T

    def start_col(k):
        return sum(WIDTHS[:k])

    def forward(k):
        n = WIDTHS[k]

        @pl.loop(0, 4)
        def _(i):
            rows = pl.ds(pl.multiple_of(i * 256, 256), 256)
            gu = jnp.dot(tok[rows, :], w[k][...].reshape(D, n), preferred_element_type=f32) * MULT
            if k < 3:
                h = hid[rows, pl.ds(pl.multiple_of((c + k) * 128, 128), 128)].astype(f32)
                gate, upw = gu[:, :128], gu[:, 128:]
            else:
                h = hid[rows, pl.ds(pl.multiple_of((1 - c) * 384, 128), 128)].astype(f32)
                gate, upw = gu, pltpu.roll(gu, 64, 1)
            s = jax.nn.sigmoid(gate)
            d_gate = h * upw * s * (1.0 + gate * (1.0 - s))
            d_up = h * gate * s
            if k < 3:
                branch[rows, pl.ds(start_col(k), 128)] = d_gate.astype(bf16)
                branch[rows, pl.ds(start_col(k) + 128, 128)] = d_up.astype(bf16)
            else:
                first = lax.broadcasted_iota(jnp.int32, gu.shape, 1) < 64
                own = jnp.logical_xor(first, jnp.broadcast_to(c == 1, gu.shape))
                mixed = jnp.where(own, d_gate, pltpu.roll(d_up, 64, 1))
                branch[rows, pl.ds(start_col(k), 128)] = mixed.astype(bf16)

    def gradient(k, base):
        n = WIDTHS[k]

        @pl.loop(0, 8)
        def _(i):
            unit = base + i // 2
            part = pl.multiple_of((i % 2) * 256, 256)
            rows = pl.ds(pl.multiple_of(unit * UNIT + part, 256), 256)
            got = jnp.dot(tok_t[rows, :], branch[:, pl.ds(start_col(k), n)], preferred_element_type=f32)
            g[k][unit, pl.ds(part, 256), :] = (got * MULT).astype(bf16)

    red = [{} for _ in range(NCHUNK)]

    def rs_y(k):
        theirs = pl.ds((1 - y_lo) * 4, 4)
        red[k]["yA"] = send(g[k].at[theirs, A], yr[k].at[:, A], up)
        red[k]["yB"] = send(g[k].at[theirs, B], yr[k].at[:, B], down)

    def rs_x1(k):
        red[k]["yA"].wait_recv()
        red[k]["yB"].wait_recv()
        for dx in (2, -1, 1, 0):
            xx = (x + dx + 4) % 4
            g[k][y_lo * 4 + xx] = add(g[k][y_lo * 4 + xx], yr[k][xx]).astype(bf16)
            if dx == 2:
                red[k]["p"] = send(g[k].at[unit_x(2), A], x1[k].at[A], right)
                red[k]["q"] = send(g[k].at[unit_x(2), B], x1[k].at[B], left)

    def rs_x2(k):
        red[k]["p"].wait_recv()
        unit = unit_x(1)
        g[k][unit, A, :] = add(g[k][unit, A, :], x1[k][A, :]).astype(bf16)
        red[k]["right"] = send(g[k].at[unit], x2[k].at[0], right)
        red[k]["q"].wait_recv()
        unit = unit_x(-1)
        g[k][unit, B, :] = add(g[k][unit, B, :], x1[k][B, :]).astype(bf16)
        red[k]["left"] = send(g[k].at[unit], x2[k].at[1], left)

    def quarter(dz):
        return pl.ds(pl.multiple_of(((z + dz + 4) % 4) * 128, 128), 128)

    def rs_z(k):
        red[k]["right"].wait_recv()
        red[k]["left"].wait_recv()
        g[k][mine] = add(g[k][mine], x2[k][0], x2[k][1]).astype(bf16)
        for j, dz in enumerate((1, -1, 2)):
            red[k][f"z{j}"] = send(g[k].at[mine, quarter(dz)], zr[k].at[j], z_next[j])

    def rs_yh(k):
        for j in range(3):
            red[k][f"z{j}"].wait_recv()
        total = add(g[k][mine, quarter(0), :], zr[k][0], zr[k][1], zr[k][2])
        yh[k][0] = total.astype(bf16)
        red[k]["yh"] = send(yh[k].at[0], yh[k].at[1], far_y)

    def rs_back(k):
        red[k]["yh"].wait_recv()
        fin[k][quarter(0), :] = add(yh[k][0], yh[k][1]).astype(bf16)
        for j in range(3):
            part = fin[k].at[quarter(0)]
            red[k][f"f{j}"] = send(part, part, z_next[j])

    def rs_swap(k):
        for j in range(3):
            red[k][f"f{j}"].wait_recv()
        red[k]["swap"] = send(fin[k].at[other_rows], sw[k], sibling)

    def rs_done(k):
        red[k]["swap"].wait_recv()
        if k < 3:
            for part in range(2):
                here = pl.ds(part * 128, 128)
                g_out[:, cols(c, k, part)] = fin[k][my_rows, here]
                g_out[:, cols(1 - c, k, part)] = sw[k][:, here]
        else:
            own = jnp.logical_xor(low, jnp.broadcast_to(c == 1, low.shape))
            mixed, theirs = fin[k][my_rows, :].astype(f32), sw[k][...].astype(f32)
            g_out[:, 384:512] = jnp.where(own, mixed, theirs).astype(bf16)
            g_out[:, FFW + 384 : FFW + 512] = pltpu.roll(jnp.where(own, theirs, mixed), 64, 1).astype(bf16)

    ig = {}

    def ig_dot(rows, unit):
        total = None
        for k in range(NCHUNK):
            part = lax.dot_general(
                branch[rows, pl.ds(start_col(k), WIDTHS[k])], w[k][unit],
                (((1,), (1,)), ((), ())), preferred_element_type=f32,
            )
            total = part if total is None else total + part
        return total * MULT

    def group_cols(j):
        return pl.ds(j * 2048, 2048)

    def ig_theirs(j):
        @pl.loop(0, 8)
        def _(i):
            unit = j * 4 + i // 2
            row = pl.multiple_of((i % 2) * 256, 256)
            cut = pl.ds(pl.multiple_of(unit * 512, 512), 512)
            tok[pl.ds(row, 256), cut] = ig_dot(pl.ds(TOK + row, 256), unit).astype(bf16)

        ig[j] = send(tok.at[pl.ds(0, TOK), group_cols(j)], ig_in.at[:, group_cols(j)], sibling)

    def ig_mine(j):
        ig[j].wait_recv()

        @pl.loop(0, 8)
        def _(i):
            unit = j * 4 + i // 2
            row = pl.multiple_of((i % 2) * 256, 256)
            cut = pl.ds(pl.multiple_of(unit * 512, 512), 512)
            value = ig_dot(pl.ds(row, 256), unit) + ig_in[pl.ds(row, 256), cut].astype(f32)
            tok[pl.ds(TOK + row, 256), cut] = value.astype(bf16)

        ig[j, "out"] = fetch(tok.at[pl.ds(TOK, TOK), group_cols(j)], ig_out.at[:, group_cols(j)])

    ag_start(0)
    ag_start(1)
    got_tok.wait()
    transpose(0)
    ag_relay(0)
    ag_relay2(0)
    ag_start(2)
    tok_in.wait_recv()
    transpose(1)
    got_hid.wait()
    hid_in.wait_recv()
    ag_done(0)
    ag_relay(1)
    forward(0)
    gradient(0, (1 - y_lo) * 4)
    rs_y(0)
    ag_relay2(1)
    ag_start(3)
    gradient(0, y_lo * 4)
    ag_relay(2)
    rs_x1(0)
    ag_done(1)
    forward(1)
    rs_x2(0)
    ag_relay2(2)
    ag_relay(3)
    gradient(1, (1 - y_lo) * 4)
    rs_y(1)
    rs_z(0)
    gradient(1, y_lo * 4)
    ag_relay2(3)
    rs_x1(1)
    ag_done(2)
    rs_yh(0)
    forward(2)
    rs_x2(1)
    rs_back(0)
    gradient(2, (1 - y_lo) * 4)
    rs_y(2)
    rs_z(1)
    gradient(2, y_lo * 4)
    ag_done(3)
    forward(3)
    rs_x1(2)
    gradient(3, (1 - y_lo) * 4)
    rs_y(3)
    rs_yh(1)
    rs_x2(2)
    gradient(3, y_lo * 4)
    rs_swap(0)
    ig_theirs(0)
    rs_x1(3)
    rs_back(1)
    rs_z(2)
    ig_theirs(1)
    rs_x2(3)
    rs_done(0)
    rs_yh(2)
    ig_mine(0)
    rs_z(3)
    rs_swap(1)
    rs_back(2)
    ig_mine(1)
    rs_yh(3)
    rs_done(1)
    rs_swap(2)
    rs_back(3)
    rs_done(2)
    rs_swap(3)
    rs_done(3)
    ig[0, "out"].wait()
    ig[1, "out"].wait()
    for copy in sent:
        copy.wait_send()


def fused(tokens, hidden, master):
    def pair(*shape):
        return [pltpu.VMEM((3, *shape, 256), bf16), pltpu.VMEM((*shape, 128), bf16)]

    anywhere = pl.BlockSpec(memory_space=pl.ANY)
    vmem = pl.BlockSpec(memory_space=pltpu.VMEM)
    return pl.pallas_call(
        kernel,
        out_shape=[jax.ShapeDtypeStruct((TOK, D), bf16), jax.ShapeDtypeStruct((HALF, 2 * FFW), bf16)],
        in_specs=[anywhere] * 3,
        out_specs=[anywhere, vmem],
        scratch_shapes=[
            pltpu.VMEM((2 * TOK, D), bf16),
            pltpu.VMEM((D, 2 * TOK), bf16),
            pltpu.VMEM((2 * TOK, 512), bf16),
            pltpu.VMEM((HALF, 2 * FFW), f32),
            pltpu.VMEM((2 * TOK, FFW), bf16),
            pltpu.VMEM((TOK, D), bf16),
            *pair(8, UNIT),
            *pair(HALF),
            *pair(8, UNIT),
            *pair(4, UNIT),
            *pair(UNIT),
            *pair(2, UNIT),
            *pair(3, 128),
            *pair(2, 128),
            *pair(UNIT),
            *pair(HALF),
            pltpu.SemaphoreType.DMA((8,)),
            pltpu.SemaphoreType.DMA((N_SEM,)),
            pltpu.SemaphoreType.DMA((N_SEM,)),
        ],
        compiler_params=pltpu.CompilerParams(
            collective_id=0, has_side_effects=True, vmem_limit_bytes=60 * 2**20
        ),
        cost_estimate=pl.CostEstimate(flops=22_500_000_000, bytes_accessed=20_000_000, transcendentals=1_000_000),
    )(tokens, hidden, master)


def body(tokens, hidden_grad, master, moment_first, moment_second):
    input_grad, grad = fused(tokens, hidden_grad, master)
    master_next, first_next, second_next = adamw(master, moment_first, moment_second, grad.astype(f32))
    return (input_grad, master_next, first_next, second_next)


def solution(mesh):
    return jax.shard_map(
        body,
        mesh=mesh,
        in_specs=(
            P(("rep", "shard"), None),
            P(("rep", "shard"), None),
            P("shard", None),
            P("shard", None),
            P("shard", None),
        ),
        out_specs=(P(("rep", "shard"), None), P("shard", None), P("shard", None), P("shard", None)),
        check_vma=False,
    )
```

```python
import jax
import jax.numpy as jnp
from jax import lax
from jax.experimental import pallas as pl
from jax.experimental.pallas import tpu as pltpu
from jax.sharding import PartitionSpec as P

MESH = pl.DeviceIdType.MESH
bias_first = 0.999973438601
bias_second = 0.99407947078
bf16, f32 = jnp.bfloat16, jnp.float32

D, FFW, TOK = 4096, 896, 512
UNIT = 512
HALF = 256
MULT = 1.0 / 64.0
CHUNKS = ((0, 0), (1, 0), (2, 0), (3, 1))
GATHER = ((('xf', 0, 512),), (('yf', 0, 256), ('zq', 256, 256)), (('xf', 0, 128), ('zq', 128, 384)), (('xf', 0, 128), ('zq', 128, 384)))
REDUCE = ((('yf', 0, 256), ('xf', 256, 256)), (('yf', 0, 384), ('xf', 384, 128)), (('yf', 0, 384), ('xf', 384, 128)), (('yf', 0, 512),))
PLAN = (
    ('start', 0, 0), ('transpose', 0), ('transpose', 1), ('relay1', 0, 0), ('start', 1, 0),
    ('start', 1, 1), ('start', 2, 0), ('start', 2, 1), ('start', 3, 0), ('start', 3, 1),
    ('relay2', 0, 0), ('relay1', 1, 1), ('relay1', 1, 0), ('relay2', 1, 0), ('relay1', 2, 0),
    ('relay1', 2, 1), ('relay1', 3, 0), ('relay1', 3, 1), ('relay2', 1, 1), ('forward', 0),
    ('relay3', 1, 0), ('relay2', 2, 0), ('grad', 0, 0), ('relay3', 1, 1), ('pass1', 1, 1),
    ('relay2', 2, 1), ('relay2', 3, 0), ('relay2', 3, 1), ('grad', 0, 1), ('grad', 0, 2),
    ('grad', 0, 3), ('x1a', 0, 0), ('pass2', 1, 1), ('relay3', 2, 1), ('rs_x2', 0, 1),
    ('relay3', 3, 1), ('pass1', 2, 1), ('pass1', 3, 1), ('x1b', 0, 0), ('rs_x2', 0, 0),
    ('forward', 1), ('grad', 1, 0), ('x3', 0, 1), ('pass2', 2, 1), ('grad', 1, 1),
    ('pass2', 3, 1), ('grad', 1, 2), ('grad', 1, 3), ('x1a', 1, 0), ('rs_x2', 1, 1),
    ('forward', 2), ('rs_z', 0), ('grad', 2, 0), ('grad', 2, 1), ('x1b', 1, 0),
    ('rs_x2', 1, 0), ('x3', 1, 1), ('grad', 2, 2), ('grad', 2, 3), ('rs_yh', 0),
    ('x1a', 2, 0), ('rs_x2', 2, 1), ('forward', 3), ('grad', 3, 0), ('grad', 3, 1),
    ('grad', 3, 2), ('grad', 3, 3), ('ig_theirs', 0), ('rs_z', 1), ('x1b', 2, 0),
    ('rs_x2', 2, 0), ('x3', 2, 1), ('back', 0), ('x1a', 3, 0), ('ig_theirs', 1),
    ('ig_theirs', 2), ('x1b', 3, 0), ('rs_yh', 1), ('ig_theirs', 3), ('rs_z', 2),
    ('swap', 0), ('done', 0), ('rs_x2', 3, 0), ('ig_mine', 0), ('back', 1),
    ('ig_mine', 1), ('rs_z', 3), ('ig_mine', 2), ('rs_yh', 2), ('ig_mine', 3),
    ('swap', 1), ('done', 1), ('rs_yh', 3), ('back', 2), ('back', 3),
    ('swap', 2), ('done', 2), ('swap', 3), ('done', 3),
)

WIDTHS = tuple(128 if half else 256 for _, half in CHUNKS)
NCHUNK = len(CHUNKS)
N_SEM = 400


def adamw(master, moment_first, moment_second, grad):
    first_next = 0.9 * moment_first + 0.1 * grad
    second_next = 0.95 * moment_second + 0.05 * grad * grad
    corrected_one = first_next / bias_first
    corrected_two = second_next / bias_second
    update = corrected_one / (jnp.sqrt(corrected_two) + 1e-08) + 0.1 * master
    return (master - 0.01 * update, first_next, second_next)


def add(*values):
    total = values[0].astype(f32)
    for v in values[1:]:
        total = total + v.astype(f32)
    return total


def start_col(k):
    return sum(WIDTHS[:k])


def buffers(n, k):
    shapes = [(8, UNIT, n), (HALF, n), (8, UNIT, n), (4, UNIT, n), (2, UNIT, n), (2, 2, UNIT, n)]
    shapes += [(3, 128, n), (2, 128, n), (UNIT, n), (HALF, n)]
    return [pltpu.VMEM(shape, bf16) for shape in shapes]


N_BUF = 10


def kernel(tokens, hidden, master, ig_out, g_out, tok, tok_t, hid, mst, branch, ig_in, *rest):
    per_chunk = [rest[i * N_BUF : (i + 1) * N_BUF] for i in range(NCHUNK)]
    w, snd, g, yr, x1, x2, zr, yh, fin, sw = zip(*per_chunk)
    lsem, ssem, rsem = rest[NCHUNK * N_BUF :]

    rep, shard = lax.axis_index("rep"), lax.axis_index("shard")
    z, y_hi = rep // 2, rep % 2
    y_lo, x, c = shard // 8, (shard // 2) % 4, shard % 2
    y = y_hi * 2 + y_lo
    mine = y_lo * 4 + x
    across = (1 - y_lo) * 4 + x

    def device(dx=0, dy=0, dz=0, dc=0):
        xx, yy, zz, cc = (x + dx + 4) % 4, (y + dy + 4) % 4, (z + dz + 4) % 4, (c + dc) % 2
        return (zz * 2 + yy // 2, ((yy % 2) * 4 + xx) * 2 + cc)

    sibling = device(dc=1)
    right, left = device(dx=1), device(dx=-1)
    up, down = device(dy=1), device(dy=-1)
    far_y = device(dy=2)
    z_next = [device(dz=1), device(dz=-1), device(dz=2)]
    partners = [sibling, right, left, up, down, far_y] + z_next

    sent = []

    def send(src, dst, to):
        i = len(sent)
        copy = pltpu.make_async_remote_copy(
            src_ref=src, dst_ref=dst, send_sem=ssem.at[i], recv_sem=rsem.at[i],
            device_id=to, device_id_type=MESH,
        )
        copy.start()
        sent.append(copy)
        return copy

    local = []

    def fetch(src, dst):
        copy = pltpu.make_async_copy(src, dst, lsem.at[len(local)])
        copy.start()
        local.append(copy)
        return copy

    def hidden_cols(core):
        return pl.ds(pl.multiple_of(core * 384, 128), 512)

    got_master = fetch(master, mst)
    got_tok = fetch(tokens, tok.at[pl.ds(0, TOK)])
    got_hid = fetch(hidden.at[:, hidden_cols(c)], hid.at[pl.ds(0, TOK)])

    barrier = pltpu.get_barrier_semaphore()
    for p in partners:
        pl.semaphore_signal(barrier, inc=1, device_id=p, device_id_type=MESH)
    pl.semaphore_wait(barrier, len(partners))

    my_rows = pl.ds(pl.multiple_of(c * HALF, HALF), HALF)
    other_rows = pl.ds(pl.multiple_of((1 - c) * HALF, HALF), HALF)

    def block_of(core, k):
        b = CHUNKS[k][0]
        return 3 if b == 3 else core * 4 + b

    def cols(core, k, part):
        return pl.ds(pl.multiple_of(part * FFW + block_of(core, k) * 128, 128), 128)

    def side(core, k):
        return core if CHUNKS[k][0] == 3 else CHUNKS[k][1] - 1

    def gate_lanes(core, k, shape):
        low = lax.broadcasted_iota(jnp.int32, shape, 1) < 64
        return jnp.logical_xor(low, jnp.broadcast_to(side(core, k) == 1, shape))

    def chunk_of(core, k):
        gate, upw = mst[:, cols(core, k, 0)], mst[:, cols(core, k, 1)]
        if CHUNKS[k][1]:
            return [jnp.where(gate_lanes(core, k, gate.shape), gate, pltpu.roll(upw, 64, 1)).astype(bf16)]
        return [gate.astype(bf16), upw.astype(bf16)]

    got_master.wait()
    swapped = []
    for k in range(NCHUNK):
        for i, (ours, others) in enumerate(zip(chunk_of(c, k), chunk_of(1 - c, k))):
            w[k][mine, my_rows, pl.ds(i * 128, 128)] = ours
            snd[k][:, pl.ds(i * 128, 128)] = others
        swapped.append(send(snd[k], w[k].at[mine, my_rows], sibling))
    tok_in = send(tokens, tok.at[pl.ds(TOK, TOK)], sibling)
    hid_in = send(hidden.at[:, hidden_cols(1 - c)], hid.at[pl.ds(TOK, TOK)], sibling)

    def unit_x(dx):
        return y_lo * 4 + (x + dx + 4) % 4

    gat = {}
    theirs4 = pl.ds((1 - y_lo) * 4, 4)

    def relay(k, unit, rows, to):
        part = w[k].at[unit, rows]
        return send(part, part, to)

    class Rows:
        def __init__(self, k, m):
            self.mode, base, size = GATHER[k][m]
            self.base, self.size = base, size
            if self.mode == "zq":
                size = size // 4
                base = base + z * size
            step = size // 2
            align = 16
            self.all = pl.ds(pl.multiple_of(base, align), size)
            self.a = pl.ds(pl.multiple_of(base, align), step)
            self.b = pl.ds(pl.multiple_of(base + step, align), step)

        def along_z(self, dz, second):
            step = self.size // 8
            first = self.base + ((z + dz + 4) % 4) * (self.size // 4) + second * step
            return pl.ds(pl.multiple_of(first, 16), step)

    part_of = {(k, m): Rows(k, m) for k in range(NCHUNK) for m in range(len(GATHER[k]))}

    def to_y(k, m, name, unit):
        r = part_of[k, m]
        gat[k, m, name] = (relay(k, unit, r.a, up), relay(k, unit, r.b, down))

    def to_z(k, m, name, unit):
        r = part_of[k, m]
        gat[k, m, name] = (relay(k, unit, r.all, z_next[0]), relay(k, unit, r.all, z_next[1]))

    def on_z(k, m, name, unit):
        r = part_of[k, m]
        gat[k, m, name][0].wait_recv()
        first = relay(k, unit, r.along_z(-1, 0), z_next[0])
        gat[k, m, name][1].wait_recv()
        gat[k, m, name + "f"] = (first, relay(k, unit, r.along_z(1, 1), z_next[1]))

    def landed(k, m, *names):
        for name in names:
            for copy in gat[k, m, name]:
                copy.wait_recv()

    def both_x(k, m, name, unit):
        r = part_of[k, m]
        gat[k, m, name] = (relay(k, unit, r.all, right), relay(k, unit, r.all, left))

    def on_x(k, m, name, row):
        r = part_of[k, m]
        gat[k, m, name][0].wait_recv()
        first = relay(k, row * 4 + (x + 3) % 4, r.a, right)
        gat[k, m, name][1].wait_recv()
        gat[k, m, name + "f"] = (first, relay(k, row * 4 + (x + 1) % 4, r.b, left))

    def start(k, m):
        if m == 0:
            swapped[k].wait_recv()
        if part_of[k, m].mode == "yf":
            to_y(k, m, "y", mine)
            both_x(k, m, "x", mine)
        else:
            both_x(k, m, "x", mine)
            to_y(k, m, "y0", mine)

    def relay1(k, m):
        mode = part_of[k, m].mode
        if mode == "yf":
            landed(k, m, "y")
            both_x(k, m, "o", across)
            return
        on_x(k, m, "x", y_lo)
        to_y(k, m, "y1", unit_x(-1))
        to_y(k, m, "y2", unit_x(1))
        if mode == "zq":
            to_z(k, m, "z1", unit_x(-1))
            to_z(k, m, "z2", unit_x(1))

    def relay2(k, m):
        mode = part_of[k, m].mode
        if mode == "yf":
            on_x(k, m, "x", y_lo)
            return
        landed(k, m, "xf")
        to_y(k, m, "y3", unit_x(2))
        if mode == "zq":
            to_z(k, m, "z3", unit_x(2))

    def relay3(k, m):
        if part_of[k, m].mode == "yf":
            on_x(k, m, "o", 1 - y_lo)
            return
        landed(k, m, "y0", "y1", "y2", "y3")
        to_z(k, m, "z4", theirs4)

    def pass1(k, m):
        on_z(k, m, "z1", unit_x(-1))
        on_z(k, m, "z2", unit_x(1))
        on_z(k, m, "z3", unit_x(2))

    def pass2(k, m):
        on_z(k, m, "z4", theirs4)

    def gathered(k):
        for m in range(len(GATHER[k])):
            mode = part_of[k, m].mode
            if mode == "yf":
                landed(k, m, "xf", "of")
            elif mode == "xf":
                landed(k, m, "y0", "y1", "y2", "y3")
            else:
                landed(k, m, "z1f", "z2f", "z3f", "z4f")

    def transpose(half):
        (got_tok.wait, tok_in.wait_recv)[half]()

        @pl.loop(0, 8)
        def _(i):
            cut = pl.ds(pl.multiple_of(i * 512, 512), 512)
            tok_t[cut, pl.ds(half * TOK, TOK)] = tok[pl.ds(half * TOK, TOK), cut].T

        if half == 1:
            got_hid.wait()
            hid_in.wait_recv()

    def forward(k):
        gathered(k)
        n, here = WIDTHS[k], start_col(k)
        block = CHUNKS[k][0]
        at = (1 - c) * 384 if block == 3 else (c + block) * 128

        @pl.loop(0, 4)
        def _(i):
            rows = pl.ds(pl.multiple_of(i * 256, 256), 256)
            gu = jnp.dot(tok[rows, :], w[k][...].reshape(D, n), preferred_element_type=f32) * MULT
            h = hid[rows, pl.ds(pl.multiple_of(at, 128), 128)].astype(f32)
            half = CHUNKS[k][1]
            gate, upw = (gu, pltpu.roll(gu, 64, 1)) if half else (gu[:, :128], gu[:, 128:])
            s = jax.nn.sigmoid(gate)
            d_gate = h * upw * s * (1.0 + gate * (1.0 - s))
            d_up = h * gate * s
            if half:
                mixed = jnp.where(gate_lanes(c, k, gu.shape), d_gate, pltpu.roll(d_up, 64, 1))
                branch[rows, pl.ds(here, 128)] = mixed.astype(bf16)
            else:
                branch[rows, pl.ds(here, 128)] = d_gate.astype(bf16)
                branch[rows, pl.ds(here + 128, 128)] = d_up.astype(bf16)

    red = {}

    def in_turn(j):
        return (x + 2 + j) % 4

    def halves(base, size):
        return pl.ds(base, size // 2), pl.ds(base + size // 2, size // 2)

    def grad(k, j):
        n = WIDTHS[k]

        @pl.loop(0, 4)
        def _(i):
            unit = ((i // 2 + 1 - y_lo) % 2) * 4 + in_turn(j)
            part = pl.multiple_of((i % 2) * 256, 256)
            rows = pl.ds(pl.multiple_of(unit * UNIT + part, 256), 256)
            got = jnp.dot(tok_t[rows, :], branch[:, pl.ds(start_col(k), n)], preferred_element_type=f32)
            g[k][unit, pl.ds(part, 256), :] = (got * MULT).astype(bf16)

        for m, (mode, base, size) in enumerate(REDUCE[k]):
            a, b = halves(base, size)
            if mode == "yf":
                unit = (1 - y_lo) * 4 + in_turn(j)
                red[k, m, "y", j] = (
                    send(g[k].at[unit, a], yr[k].at[in_turn(j), a], up),
                    send(g[k].at[unit, b], yr[k].at[in_turn(j), b], down),
                )
            elif j == 0:
                red[k, m, "x1"] = [
                    (send(g[k].at[u * 4 + in_turn(0), a], x1[k].at[u, a], right),
                     send(g[k].at[u * 4 + in_turn(0), b], x1[k].at[u, b], left))
                    for u in range(2)
                ]

    def plus(k, unit, rows, *others):
        g[k][unit, rows, :] = add(g[k][unit, rows, :], *others).astype(bf16)

    def take_y(k, m, j):
        _, base, size = REDUCE[k][m]
        for copy in red[k, m, "y", j]:
            copy.wait_recv()
        rows = pl.ds(base, size)
        plus(k, y_lo * 4 + in_turn(j), rows, yr[k][in_turn(j), rows, :])

    def x1a(k, m):
        _, base, size = REDUCE[k][m]
        a, b = halves(base, size)
        take_y(k, m, 0)
        red[k, m, "p"] = send(g[k].at[unit_x(2), a], x1[k].at[0, a], right)
        red[k, m, "q"] = send(g[k].at[unit_x(2), b], x1[k].at[0, b], left)

    def x1b(k, m):
        for j in range(1, 4):
            take_y(k, m, j)

    def rs_x2(k, m):
        mode, base, size = REDUCE[k][m]
        rows, (a, b) = pl.ds(base, size), halves(base, size)
        if mode == "yf":
            red[k, m, "p"].wait_recv()
            plus(k, unit_x(1), a, x1[k][0, a, :])
            red[k, m, "r"] = [send(g[k].at[unit_x(1), rows], x2[k].at[0, 0, rows], right)]
            red[k, m, "q"].wait_recv()
            plus(k, unit_x(-1), b, x1[k][0, b, :])
            red[k, m, "l"] = [send(g[k].at[unit_x(-1), rows], x2[k].at[1, 0, rows], left)]
            return
        red[k, m, "r"], red[k, m, "l"] = [], []
        for u in range(2):
            p, q = red[k, m, "x1"][u]
            here = u * 4 + (x + 1) % 4
            p.wait_recv()
            plus(k, here, a, x1[k][u, a, :])
            red[k, m, "r"].append(send(g[k].at[here, rows], x2[k].at[0, u, rows], right))
            here = u * 4 + (x + 3) % 4
            q.wait_recv()
            plus(k, here, b, x1[k][u, b, :])
            red[k, m, "l"].append(send(g[k].at[here, rows], x2[k].at[1, u, rows], left))

    def x3(k, m):
        _, base, size = REDUCE[k][m]
        rows, (a, b) = pl.ds(base, size), halves(base, size)
        for copy in red[k, m, "r"] + red[k, m, "l"]:
            copy.wait_recv()
        for u in range(2):
            plus(k, u * 4 + x, rows, x2[k][0, u, rows, :], x2[k][1, u, rows, :])
        red[k, m, "ya"] = (
            send(g[k].at[across, a], yr[k].at[0, a], up),
            send(g[k].at[across, b], yr[k].at[0, b], down),
        )

    def quarter(dz):
        return pl.ds(pl.multiple_of(((z + dz + 4) % 4) * 128, 128), 128)

    def rs_z(k):
        for m, (mode, base, size) in enumerate(REDUCE[k]):
            rows = pl.ds(base, size)
            if mode == "yf":
                for copy in red[k, m, "r"] + red[k, m, "l"]:
                    copy.wait_recv()
                plus(k, mine, rows, x2[k][0, 0, rows, :], x2[k][1, 0, rows, :])
            else:
                for copy in red[k, m, "ya"]:
                    copy.wait_recv()
                plus(k, mine, rows, yr[k][0, rows, :])
        red[k, "z"] = [send(g[k].at[mine, quarter(dz)], zr[k].at[j], z_next[j]) for j, dz in enumerate((1, -1, 2))]

    def rs_yh(k):
        for copy in red[k, "z"]:
            copy.wait_recv()
        total = add(g[k][mine, quarter(0), :], zr[k][0], zr[k][1], zr[k][2])
        yh[k][0] = total.astype(bf16)
        red[k, "yh"] = send(yh[k].at[0], yh[k].at[1], far_y)

    def back(k):
        red[k, "yh"].wait_recv()
        fin[k][quarter(0), :] = add(yh[k][0], yh[k][1]).astype(bf16)
        part = fin[k].at[quarter(0)]
        red[k, "back"] = [send(part, part, z_next[j]) for j in range(3)]

    def swap(k):
        for copy in red[k, "back"]:
            copy.wait_recv()
        red[k, "swap"] = send(fin[k].at[other_rows], sw[k], sibling)

    def done(k):
        red[k, "swap"].wait_recv()
        own, theirs = fin[k][my_rows, :], sw[k][...]
        block, half = CHUNKS[k]
        if not half:
            for core, value in ((c, own), (1 - c, theirs)):
                g_out[:, cols(core, k, 0)] = value[:, :128]
                g_out[:, cols(core, k, 1)] = value[:, 128:]
            return
        gates = gate_lanes(c, k, own.shape)
        if block == 3:
            g_out[:, cols(c, k, 0)] = jnp.where(gates, own, theirs)
            g_out[:, cols(c, k, 1)] = pltpu.roll(jnp.where(gates, theirs, own).astype(f32), 64, 1).astype(bf16)
            return
        for core, value in ((c, own), (1 - c, theirs)):
            for part, lanes in ((0, value), (1, pltpu.roll(value.astype(f32), 64, 1).astype(bf16))):
                if half == 2:
                    lanes = jnp.where(gates, lanes, g_out[:, cols(core, k, part)])
                g_out[:, cols(core, k, part)] = lanes

    ig = {}

    def ig_dot(rows, unit):
        total = None
        for k in range(NCHUNK):
            part = lax.dot_general(
                branch[rows, pl.ds(start_col(k), WIDTHS[k])], w[k][unit],
                (((1,), (1,)), ((), ())), preferred_element_type=f32,
            )
            total = part if total is None else total + part
        return total * MULT

    def group_cols(j):
        return pl.ds(j * 1024, 1024)

    def ig_theirs(j):
        @pl.loop(0, 4)
        def _(i):
            unit = j * 2 + i // 2
            row = pl.multiple_of((i % 2) * 256, 256)
            cut = pl.ds(pl.multiple_of(unit * 512, 512), 512)
            tok[pl.ds(row, 256), cut] = ig_dot(pl.ds(TOK + row, 256), unit).astype(bf16)

        ig[j] = send(tok.at[pl.ds(0, TOK), group_cols(j)], ig_in.at[:, group_cols(j)], sibling)

    def ig_mine(j):
        ig[j].wait_recv()

        @pl.loop(0, 4)
        def _(i):
            unit = j * 2 + i // 2
            row = pl.multiple_of((i % 2) * 256, 256)
            cut = pl.ds(pl.multiple_of(unit * 512, 512), 512)
            value = ig_dot(pl.ds(row, 256), unit) + ig_in[pl.ds(row, 256), cut].astype(f32)
            tok[pl.ds(TOK + row, 256), cut] = value.astype(bf16)

        ig[j, "out"] = fetch(tok.at[pl.ds(TOK, TOK), group_cols(j)], ig_out.at[:, group_cols(j)])

    steps = dict(
        start=start, relay1=relay1, relay2=relay2, relay3=relay3, pass1=pass1, pass2=pass2, transpose=transpose,
        forward=forward, grad=grad, x1a=x1a, x1b=x1b, rs_x2=rs_x2, x3=x3, rs_z=rs_z, rs_yh=rs_yh, back=back,
        swap=swap, done=done, ig_theirs=ig_theirs, ig_mine=ig_mine,
    )
    for name, *which in PLAN:
        steps[name](*which)
    for j in range(4):
        ig[j, "out"].wait()
    for copy in sent:
        copy.wait_send()


def fused(tokens, hidden, master):
    anywhere = pl.BlockSpec(memory_space=pl.ANY)
    vmem = pl.BlockSpec(memory_space=pltpu.VMEM)
    return pl.pallas_call(
        kernel,
        out_shape=[jax.ShapeDtypeStruct((TOK, D), bf16), jax.ShapeDtypeStruct((HALF, 2 * FFW), bf16)],
        in_specs=[anywhere] * 3,
        out_specs=[anywhere, vmem],
        scratch_shapes=[
            pltpu.VMEM((2 * TOK, D), bf16),
            pltpu.VMEM((D, 2 * TOK), bf16),
            pltpu.VMEM((2 * TOK, 512), bf16),
            pltpu.VMEM((HALF, 2 * FFW), f32),
            pltpu.VMEM((2 * TOK, FFW), bf16),
            pltpu.VMEM((TOK, D), bf16),
            *(ref for k in range(NCHUNK) for ref in buffers(WIDTHS[k], k)),
            pltpu.SemaphoreType.DMA((8,)),
            pltpu.SemaphoreType.DMA((N_SEM,)),
            pltpu.SemaphoreType.DMA((N_SEM,)),
        ],
        compiler_params=pltpu.CompilerParams(
            collective_id=0, has_side_effects=True, vmem_limit_bytes=63 * 2**20
        ),
        cost_estimate=pl.CostEstimate(flops=22_500_000_000, bytes_accessed=20_000_000, transcendentals=1_000_000),
    )(tokens, hidden, master)


def body(tokens, hidden_grad, master, moment_first, moment_second):
    input_grad, grad = fused(tokens, hidden_grad, master)
    master_next, first_next, second_next = adamw(master, moment_first, moment_second, grad.astype(f32))
    return (input_grad, master_next, first_next, second_next)


def solution(mesh):
    return jax.shard_map(
        body,
        mesh=mesh,
        in_specs=(
            P(("rep", "shard"), None),
            P(("rep", "shard"), None),
            P("shard", None),
            P("shard", None),
            P("shard", None),
        ),
        out_specs=(P(("rep", "shard"), None), P("shard", None), P("shard", None), P("shard", None)),
        check_vma=False,
    )
```

```python
import math

import jax
import jax.numpy as jnp
from jax import lax
from jax.experimental import pallas as pl
from jax.experimental.pallas import tpu as pltpu
from jax.sharding import PartitionSpec as P

MESH = pl.DeviceIdType.MESH
bias_first = 0.999973438601
bias_second = 0.99407947078
bf16, f32 = jnp.bfloat16, jnp.float32

D, FFW, TOK = 4096, 896, 512
UNIT = 512
HALF = 256
MULT = 1.0 / 64.0
CHUNKS = ((0, 0), (1, 0), (2, 0), (3, 1))
GATHER = ((('xf', 0, 512),), (('yf', 0, 256), ('zq', 256, 256)), (('xf', 0, 128), ('zq', 128, 384)), (('xf', 0, 128), ('zq', 128, 384)))
REDUCE = ((('yf', 0, 256), ('xf', 256, 256)), (('yf', 0, 384), ('xf', 384, 128)), (('yf', 0, 384), ('xf', 384, 128)), (('yf', 0, 512),))
PLAN = (
    ('start', 0, 0), ('transpose', 0), ('transpose', 1), ('relay1', 0, 0), ('start', 1, 0),
    ('start', 1, 1), ('start', 2, 0), ('start', 2, 1), ('start', 3, 0), ('start', 3, 1),
    ('relay2', 0, 0), ('relay1', 1, 1), ('relay1', 1, 0), ('relay2', 1, 0), ('relay1', 2, 0),
    ('relay1', 2, 1), ('relay1', 3, 0), ('relay1', 3, 1), ('relay2', 1, 1), ('forward', 0),
    ('relay3', 1, 0), ('relay2', 2, 0), ('grad', 0, 0), ('relay3', 1, 1), ('pass1', 1, 1),
    ('relay2', 2, 1), ('relay2', 3, 0), ('relay2', 3, 1), ('grad', 0, 1), ('grad', 0, 2),
    ('grad', 0, 3), ('x1a', 0, 0), ('pass2', 1, 1), ('relay3', 2, 1), ('rs_x2', 0, 1),
    ('relay3', 3, 1), ('pass1', 2, 1), ('pass1', 3, 1), ('x1b', 0, 0), ('rs_x2', 0, 0),
    ('forward', 1), ('grad', 1, 0), ('x3', 0, 1), ('pass2', 2, 1), ('grad', 1, 1),
    ('pass2', 3, 1), ('grad', 1, 2), ('grad', 1, 3), ('x1a', 1, 0), ('rs_x2', 1, 1),
    ('forward', 2), ('rs_z', 0), ('grad', 2, 0), ('grad', 2, 1), ('x1b', 1, 0),
    ('rs_x2', 1, 0), ('x3', 1, 1), ('grad', 2, 2), ('grad', 2, 3), ('rs_yh', 0),
    ('x1a', 2, 0), ('rs_x2', 2, 1), ('forward', 3), ('grad', 3, 0), ('grad', 3, 1),
    ('grad', 3, 2), ('grad', 3, 3), ('ig_theirs', 0), ('rs_z', 1), ('x1b', 2, 0),
    ('rs_x2', 2, 0), ('x3', 2, 1), ('back', 0), ('x1a', 3, 0), ('ig_theirs', 1),
    ('ig_theirs', 2), ('x1b', 3, 0), ('rs_yh', 1), ('ig_theirs', 3), ('rs_z', 2),
    ('swap', 0), ('done', 0), ('rs_x2', 3, 0), ('ig_mine', 0), ('back', 1),
    ('ig_mine', 1), ('rs_z', 3), ('ig_mine', 2), ('rs_yh', 2), ('ig_mine', 3),
    ('swap', 1), ('done', 1), ('rs_yh', 3), ('back', 2), ('back', 3),
    ('swap', 2), ('done', 2), ('swap', 3), ('done', 3),
)

WIDTHS = tuple(128 if half else 256 for _, half in CHUNKS)
NCHUNK = len(CHUNKS)
N_IN, N_OUT = 90, 7


def adamw(master, moment_first, moment_second, grad):
    first_next = 0.9 * moment_first + 0.1 * grad
    second_next = 0.95 * moment_second + 0.05 * grad * grad
    corrected_one = first_next / bias_first
    corrected_two = second_next / bias_second
    update = corrected_one / (jnp.sqrt(corrected_two) + 1e-08) + 0.1 * master
    return (master - 0.01 * update, first_next, second_next)


def add(*values):
    total = values[0].astype(f32)
    for v in values[1:]:
        total = total + v.astype(f32)
    return total


def start_col(k):
    return sum(WIDTHS[:k])


def buffers(n, k):
    shapes = [(8, UNIT, n), (HALF, n), (8, UNIT, n), (4, UNIT, n), (2, UNIT, n), (2, 2, UNIT, n)]
    shapes += [(3, 128, n), (2, 128, n), (UNIT, n), (HALF, n)]
    return [pltpu.VMEM(shape, bf16) for shape in shapes]


N_BUF = 10


def kernel(tokens, hidden, master, ig_out, g_out, tok, tok_t, hid, mst, branch, ig_in, *rest):
    per_chunk = [rest[i * N_BUF : (i + 1) * N_BUF] for i in range(NCHUNK)]
    w, snd, g, yr, x1, x2, zr, yh, fin, sw = zip(*per_chunk)
    lsem, ssem, rsem = rest[NCHUNK * N_BUF :]

    rep, shard = lax.axis_index("rep"), lax.axis_index("shard")
    z, y_hi = rep // 2, rep % 2
    y_lo, x, c = shard // 8, (shard // 2) % 4, shard % 2
    y = y_hi * 2 + y_lo
    mine = y_lo * 4 + x
    across = (1 - y_lo) * 4 + x

    def device(dx=0, dy=0, dz=0, dc=0):
        xx, yy, zz, cc = (x + dx + 4) % 4, (y + dy + 4) % 4, (z + dz + 4) % 4, (c + dc) % 2
        return (zz * 2 + yy // 2, ((yy % 2) * 4 + xx) * 2 + cc)

    sibling = device(dc=1)
    right, left = device(dx=1), device(dx=-1)
    up, down = device(dy=1), device(dy=-1)
    far_y = device(dy=2)
    z_next = [device(dz=1), device(dz=-1), device(dz=2)]
    partners = [sibling, right, left, up, down, far_y] + z_next

    def cut_of(size):
        tiles, left_over = divmod(size, 16 * 128 * 2)
        fits = [wide for wide in range(1, 9) if tiles % wide == 0 and tiles // wide <= D // 16]
        return (tiles // fits[-1] * 16, fits[-1] * 128) if fits and not left_over else None

    def some_bytes(size):
        rows, columns = cut_of(size)
        return tok_t.at[pl.ds(0, rows), pl.ds(0, columns)]

    outgoing, inboxes = [], []

    def awaiting(size, out, into):
        ref = some_bytes(size)
        return pltpu.make_async_remote_copy(
            src_ref=ref, dst_ref=ref, send_sem=ssem.at[out], recv_sem=rsem.at[into],
            device_id=sibling, device_id_type=MESH,
        )

    class Inbox:
        def __init__(self):
            self.index, self.size, self.waited = len(inboxes), 0, False
            inboxes.append(self)

        def wait_recv(self):
            assert self.size and not self.waited
            self.waited = True
            awaiting(self.size, 0, self.index).wait_recv()

    def send(src, dst, to, into=None):
        into = Inbox() if into is None else into
        size = 2 * math.prod(src.shape)
        if not outgoing or (outgoing[-1] > 3 * 2**20 and cut_of(outgoing[-1])):
            outgoing.append(0)
        outgoing[-1] += size
        into.size += size
        pltpu.make_async_remote_copy(
            src_ref=src, dst_ref=dst, send_sem=ssem.at[len(outgoing) - 1], recv_sem=rsem.at[into.index],
            device_id=to, device_id_type=MESH,
        ).start()
        return into

    local = []

    def fetch(src, dst):
        copy = pltpu.make_async_copy(src, dst, lsem.at[len(local)])
        copy.start()
        local.append(copy)
        return copy

    def hidden_cols(core):
        return pl.ds(pl.multiple_of(core * 384, 128), 512)

    got_master = fetch(master, mst)
    got_tok = fetch(tokens, tok.at[pl.ds(0, TOK)])
    got_hid = fetch(hidden.at[:, hidden_cols(c)], hid.at[pl.ds(0, TOK)])

    barrier = pltpu.get_barrier_semaphore()
    for p in partners:
        pl.semaphore_signal(barrier, inc=1, device_id=p, device_id_type=MESH)
    pl.semaphore_wait(barrier, len(partners))

    my_rows = pl.ds(pl.multiple_of(c * HALF, HALF), HALF)
    other_rows = pl.ds(pl.multiple_of((1 - c) * HALF, HALF), HALF)

    def block_of(core, k):
        b = CHUNKS[k][0]
        return 3 if b == 3 else core * 4 + b

    def cols(core, k, part):
        return pl.ds(pl.multiple_of(part * FFW + block_of(core, k) * 128, 128), 128)

    def side(core, k):
        return core if CHUNKS[k][0] == 3 else CHUNKS[k][1] - 1

    def gate_lanes(core, k, shape):
        low = lax.broadcasted_iota(jnp.int32, shape, 1) < 64
        return jnp.logical_xor(low, jnp.broadcast_to(side(core, k) == 1, shape))

    def chunk_of(core, k):
        gate, upw = mst[:, cols(core, k, 0)], mst[:, cols(core, k, 1)]
        if CHUNKS[k][1]:
            return [jnp.where(gate_lanes(core, k, gate.shape), gate, pltpu.roll(upw, 64, 1)).astype(bf16)]
        return [gate.astype(bf16), upw.astype(bf16)]

    got_master.wait()
    swapped = []
    for k in range(NCHUNK):
        for i, (ours, others) in enumerate(zip(chunk_of(c, k), chunk_of(1 - c, k))):
            w[k][mine, my_rows, pl.ds(i * 128, 128)] = ours
            snd[k][:, pl.ds(i * 128, 128)] = others
        swapped.append(send(snd[k], w[k].at[mine, my_rows], sibling))
    tok_in = send(tokens, tok.at[pl.ds(TOK, TOK)], sibling)
    hid_in = send(hidden.at[:, hidden_cols(1 - c)], hid.at[pl.ds(TOK, TOK)], sibling)

    def unit_x(dx):
        return y_lo * 4 + (x + dx + 4) % 4

    gat = {}
    theirs4 = pl.ds((1 - y_lo) * 4, 4)

    def relay(k, unit, rows, to, into):
        part = w[k].at[unit, rows]
        send(part, part, to, into)

    def inbox(*key):
        if key not in gat:
            gat[key] = Inbox()
        return gat[key]

    class Rows:
        def __init__(self, k, m):
            self.mode, base, size = GATHER[k][m]
            self.base, self.size = base, size
            if self.mode == "zq":
                size = size // 4
                base = base + z * size
            step = size // 2
            align = 16
            self.all = pl.ds(pl.multiple_of(base, align), size)
            self.a = pl.ds(pl.multiple_of(base, align), step)
            self.b = pl.ds(pl.multiple_of(base + step, align), step)

        def along_z(self, dz, second):
            step = self.size // 8
            first = self.base + ((z + dz + 4) % 4) * (self.size // 4) + second * step
            return pl.ds(pl.multiple_of(first, 16), step)

    part_of = {(k, m): Rows(k, m) for k in range(NCHUNK) for m in range(len(GATHER[k]))}

    def to_y(k, m, name, unit):
        r = part_of[k, m]
        relay(k, unit, r.a, up, inbox(k, m, name))
        relay(k, unit, r.b, down, inbox(k, m, name))

    def to_z(k, m, name, unit):
        r = part_of[k, m]
        for there in z_next[:2]:
            relay(k, unit, r.all, there, inbox(k, m, name))

    def on_z(k, m, unit):
        r = part_of[k, m]
        relay(k, unit, r.along_z(-1, 0), z_next[0], inbox(k, m, "zf"))
        relay(k, unit, r.along_z(1, 1), z_next[1], inbox(k, m, "zf"))

    def landed(*key):
        gat[key].wait_recv()

    def both_x(k, m, name, unit):
        r = part_of[k, m]
        for there in (right, left):
            relay(k, unit, r.all, there, inbox(k, m, name))

    def on_x(k, m, name, row):
        r = part_of[k, m]
        landed(k, m, name)
        relay(k, row * 4 + (x + 3) % 4, r.a, right, inbox(k, m, "xf"))
        relay(k, row * 4 + (x + 1) % 4, r.b, left, inbox(k, m, "xf"))

    def start(k, m):
        if m == 0:
            swapped[k].wait_recv()
        if part_of[k, m].mode == "yf":
            to_y(k, m, "y", mine)
            both_x(k, m, "x", mine)
        else:
            both_x(k, m, "x", mine)
            to_y(k, m, "y", mine)

    def relay1(k, m):
        mode = part_of[k, m].mode
        if mode == "yf":
            landed(k, m, "y")
            both_x(k, m, "o", across)
            return
        on_x(k, m, "x", y_lo)
        for dx in (-1, 1):
            to_y(k, m, "y", unit_x(dx))
            if mode == "zq":
                to_z(k, m, "z", unit_x(dx))

    def relay2(k, m):
        mode = part_of[k, m].mode
        if mode == "yf":
            on_x(k, m, "x", y_lo)
            return
        landed(k, m, "xf")
        to_y(k, m, "y", unit_x(2))
        if mode == "zq":
            to_z(k, m, "z", unit_x(2))

    def relay3(k, m):
        if part_of[k, m].mode == "yf":
            on_x(k, m, "o", 1 - y_lo)
            return
        landed(k, m, "y")
        to_z(k, m, "z4", theirs4)

    def pass1(k, m):
        landed(k, m, "z")
        for dx in (-1, 1, 2):
            on_z(k, m, unit_x(dx))

    def pass2(k, m):
        landed(k, m, "z4")
        on_z(k, m, theirs4)

    def gathered(k):
        for m in range(len(GATHER[k])):
            landed(k, m, {"yf": "xf", "xf": "y", "zq": "zf"}[part_of[k, m].mode])

    def transpose(half):
        (got_tok.wait, tok_in.wait_recv)[half]()

        @pl.loop(0, 8)
        def _(i):
            cut = pl.ds(pl.multiple_of(i * 512, 512), 512)
            tok_t[cut, pl.ds(half * TOK, TOK)] = tok[pl.ds(half * TOK, TOK), cut].T

        if half == 1:
            got_hid.wait()
            hid_in.wait_recv()

    def forward(k):
        gathered(k)
        n, here = WIDTHS[k], start_col(k)
        block = CHUNKS[k][0]
        at = (1 - c) * 384 if block == 3 else (c + block) * 128

        @pl.loop(0, 2)
        def _(i):
            rows = pl.ds(pl.multiple_of(i * 512, 512), 512)
            gu = jnp.dot(tok[rows, :], w[k][...].reshape(D, n), preferred_element_type=f32) * MULT
            h = hid[rows, pl.ds(pl.multiple_of(at, 128), 128)].astype(f32)
            half = CHUNKS[k][1]
            gate, upw = (gu, pltpu.roll(gu, 64, 1)) if half else (gu[:, :128], gu[:, 128:])
            s = jax.nn.sigmoid(gate)
            d_gate = h * upw * s * (1.0 + gate * (1.0 - s))
            d_up = h * gate * s
            if half:
                mixed = jnp.where(gate_lanes(c, k, gu.shape), d_gate, pltpu.roll(d_up, 64, 1))
                branch[rows, pl.ds(here, 128)] = mixed.astype(bf16)
            else:
                branch[rows, pl.ds(here, 128)] = d_gate.astype(bf16)
                branch[rows, pl.ds(here + 128, 128)] = d_up.astype(bf16)

    red = {}

    def in_turn(j):
        return (x + 2 + j) % 4

    def halves(base, size):
        return pl.ds(base, size // 2), pl.ds(base + size // 2, size // 2)

    def grad(k, j):
        n = WIDTHS[k]

        @pl.loop(0, 2)
        def _(i):
            unit = ((i + 1 - y_lo) % 2) * 4 + in_turn(j)
            rows = pl.ds(pl.multiple_of(unit * UNIT, UNIT), UNIT)
            got = jnp.dot(tok_t[rows, :], branch[:, pl.ds(start_col(k), n)], preferred_element_type=f32)
            g[k][unit] = (got * MULT).astype(bf16)

        for m, (mode, base, size) in enumerate(REDUCE[k]):
            a, b = halves(base, size)
            if mode == "yf":
                unit, box = (1 - y_lo) * 4 + in_turn(j), Inbox()
                send(g[k].at[unit, a], yr[k].at[in_turn(j), a], up, box)
                send(g[k].at[unit, b], yr[k].at[in_turn(j), b], down, box)
                red[k, m, "y", j] = box
            elif j == 0:
                red[k, m, "x1"] = box = Inbox()
                for u in range(2):
                    send(g[k].at[u * 4 + in_turn(0), a], x1[k].at[u, a], right, box)
                    send(g[k].at[u * 4 + in_turn(0), b], x1[k].at[u, b], left, box)

    def plus(k, unit, rows, *others):
        g[k][unit, rows, :] = add(g[k][unit, rows, :], *others).astype(bf16)

    def take_y(k, m, j):
        _, base, size = REDUCE[k][m]
        red[k, m, "y", j].wait_recv()
        rows = pl.ds(base, size)
        plus(k, y_lo * 4 + in_turn(j), rows, yr[k][in_turn(j), rows, :])

    def x1a(k, m):
        _, base, size = REDUCE[k][m]
        a, b = halves(base, size)
        take_y(k, m, 0)
        red[k, m, "x1"] = box = Inbox()
        send(g[k].at[unit_x(2), a], x1[k].at[0, a], right, box)
        send(g[k].at[unit_x(2), b], x1[k].at[0, b], left, box)

    def x1b(k, m):
        for j in range(1, 4):
            take_y(k, m, j)

    def rs_x2(k, m):
        mode, base, size = REDUCE[k][m]
        rows, (a, b) = pl.ds(base, size), halves(base, size)
        red[k, m, "x1"].wait_recv()
        red[k, m, "x2"] = box = Inbox()
        for u, row in ((0, y_lo),) if mode == "yf" else ((0, 0), (1, 1)):
            here = row * 4 + (x + 1) % 4
            plus(k, here, a, x1[k][u, a, :])
            send(g[k].at[here, rows], x2[k].at[0, u, rows], right, box)
            here = row * 4 + (x + 3) % 4
            plus(k, here, b, x1[k][u, b, :])
            send(g[k].at[here, rows], x2[k].at[1, u, rows], left, box)

    def x3(k, m):
        _, base, size = REDUCE[k][m]
        rows, (a, b) = pl.ds(base, size), halves(base, size)
        red[k, m, "x2"].wait_recv()
        for u in range(2):
            plus(k, u * 4 + x, rows, x2[k][0, u, rows, :], x2[k][1, u, rows, :])
        red[k, m, "y"] = box = Inbox()
        send(g[k].at[across, a], yr[k].at[0, a], up, box)
        send(g[k].at[across, b], yr[k].at[0, b], down, box)

    def quarter(dz):
        return pl.ds(pl.multiple_of(((z + dz + 4) % 4) * 128, 128), 128)

    def rs_z(k):
        for m, (mode, base, size) in enumerate(REDUCE[k]):
            rows = pl.ds(base, size)
            if mode == "yf":
                red[k, m, "x2"].wait_recv()
                plus(k, mine, rows, x2[k][0, 0, rows, :], x2[k][1, 0, rows, :])
            else:
                red[k, m, "y"].wait_recv()
                plus(k, mine, rows, yr[k][0, rows, :])
        red[k, "z"] = box = Inbox()
        for j, dz in enumerate((1, -1, 2)):
            send(g[k].at[mine, quarter(dz)], zr[k].at[j], z_next[j], box)

    def rs_yh(k):
        red[k, "z"].wait_recv()
        total = add(g[k][mine, quarter(0), :], zr[k][0], zr[k][1], zr[k][2])
        yh[k][0] = total.astype(bf16)
        red[k, "yh"] = send(yh[k].at[0], yh[k].at[1], far_y)

    def back(k):
        red[k, "yh"].wait_recv()
        fin[k][quarter(0), :] = add(yh[k][0], yh[k][1]).astype(bf16)
        part = fin[k].at[quarter(0)]
        red[k, "back"] = box = Inbox()
        for j in range(3):
            send(part, part, z_next[j], box)

    def swap(k):
        red[k, "back"].wait_recv()
        red[k, "swap"] = send(fin[k].at[other_rows], sw[k], sibling)

    def done(k):
        red[k, "swap"].wait_recv()
        own, theirs = fin[k][my_rows, :], sw[k][...]
        block, half = CHUNKS[k]
        if not half:
            for core, value in ((c, own), (1 - c, theirs)):
                g_out[:, cols(core, k, 0)] = value[:, :128]
                g_out[:, cols(core, k, 1)] = value[:, 128:]
            return
        gates = gate_lanes(c, k, own.shape)
        if block == 3:
            g_out[:, cols(c, k, 0)] = jnp.where(gates, own, theirs)
            g_out[:, cols(c, k, 1)] = pltpu.roll(jnp.where(gates, theirs, own).astype(f32), 64, 1).astype(bf16)
            return
        for core, value in ((c, own), (1 - c, theirs)):
            for part, lanes in ((0, value), (1, pltpu.roll(value.astype(f32), 64, 1).astype(bf16))):
                if half == 2:
                    lanes = jnp.where(gates, lanes, g_out[:, cols(core, k, part)])
                g_out[:, cols(core, k, part)] = lanes

    ig = {}

    def ig_dot(rows, unit):
        total = None
        for k in range(NCHUNK):
            part = lax.dot_general(
                branch[rows, pl.ds(start_col(k), WIDTHS[k])], w[k][unit],
                (((1,), (1,)), ((), ())), preferred_element_type=f32,
            )
            total = part if total is None else total + part
        return total * MULT

    def group_cols(j):
        return pl.ds(j * 1024, 1024)

    def ig_theirs(j):
        @pl.loop(0, 2)
        def _(i):
            unit = j * 2 + i
            cut = pl.ds(pl.multiple_of(unit * 512, 512), 512)
            tok[pl.ds(0, TOK), cut] = ig_dot(pl.ds(TOK, TOK), unit).astype(bf16)

        ig[j] = send(tok.at[pl.ds(0, TOK), group_cols(j)], ig_in.at[:, group_cols(j)], sibling)

    def ig_mine(j):
        ig[j].wait_recv()

        @pl.loop(0, 2)
        def _(i):
            unit = j * 2 + i
            cut = pl.ds(pl.multiple_of(unit * 512, 512), 512)
            value = ig_dot(pl.ds(0, TOK), unit) + ig_in[:, cut].astype(f32)
            tok[pl.ds(TOK, TOK), cut] = value.astype(bf16)

        ig[j, "out"] = fetch(tok.at[pl.ds(TOK, TOK), group_cols(j)], ig_out.at[:, group_cols(j)])

    steps = dict(
        start=start, relay1=relay1, relay2=relay2, relay3=relay3, pass1=pass1, pass2=pass2, transpose=transpose,
        forward=forward, grad=grad, x1a=x1a, x1b=x1b, rs_x2=rs_x2, x3=x3, rs_z=rs_z, rs_yh=rs_yh, back=back,
        swap=swap, done=done, ig_theirs=ig_theirs, ig_mine=ig_mine,
    )
    for name, *which in PLAN:
        steps[name](*which)
    for j in range(4):
        ig[j, "out"].wait()
    assert all(box.waited for box in inboxes) and len(inboxes) <= N_IN and len(outgoing) <= N_OUT
    for i, size in enumerate(outgoing):
        awaiting(size, i, 0).wait_send()


def fused(tokens, hidden, master):
    anywhere = pl.BlockSpec(memory_space=pl.ANY)
    vmem = pl.BlockSpec(memory_space=pltpu.VMEM)
    return pl.pallas_call(
        kernel,
        out_shape=[jax.ShapeDtypeStruct((TOK, D), bf16), jax.ShapeDtypeStruct((HALF, 2 * FFW), bf16)],
        in_specs=[anywhere] * 3,
        out_specs=[anywhere, vmem],
        scratch_shapes=[
            pltpu.VMEM((2 * TOK, D), bf16),
            pltpu.VMEM((D, 2 * TOK), bf16),
            pltpu.VMEM((2 * TOK, 512), bf16),
            pltpu.VMEM((HALF, 2 * FFW), f32),
            pltpu.VMEM((2 * TOK, FFW), bf16),
            pltpu.VMEM((TOK, D), bf16),
            *(ref for k in range(NCHUNK) for ref in buffers(WIDTHS[k], k)),
            pltpu.SemaphoreType.DMA((8,)),
            pltpu.SemaphoreType.DMA((N_OUT,)),
            pltpu.SemaphoreType.DMA((N_IN,)),
        ],
        compiler_params=pltpu.CompilerParams(
            collective_id=0, has_side_effects=True, vmem_limit_bytes=63 * 2**20
        ),
        cost_estimate=pl.CostEstimate(flops=22_500_000_000, bytes_accessed=20_000_000, transcendentals=1_000_000),
    )(tokens, hidden, master)


def body(tokens, hidden_grad, master, moment_first, moment_second):
    input_grad, grad = fused(tokens, hidden_grad, master)
    master_next, first_next, second_next = adamw(master, moment_first, moment_second, grad.astype(f32))
    return (input_grad, master_next, first_next, second_next)


def solution(mesh):
    return jax.shard_map(
        body,
        mesh=mesh,
        in_specs=(
            P(("rep", "shard"), None),
            P(("rep", "shard"), None),
            P("shard", None),
            P("shard", None),
            P("shard", None),
        ),
        out_specs=(P(("rep", "shard"), None), P("shard", None), P("shard", None), P("shard", None)),
        check_vma=False,
    )
```

```python
import math

import jax
import jax.numpy as jnp
from jax import lax
from jax.experimental import pallas as pl
from jax.experimental.pallas import tpu as pltpu
from jax.sharding import PartitionSpec as P

MESH = pl.DeviceIdType.MESH
bias_first = 0.999973438601
bias_second = 0.99407947078
bf16, f32 = jnp.bfloat16, jnp.float32

D, FFW, TOK = 4096, 896, 512
UNIT = 512
HALF = 256
MULT = 1.0 / 64.0
CHUNKS = ((3, 1), (0, 0), (1, 0), (2, 0))
FAR = (False, False, False, True)
GATHER = ((('zq', 0, 512),), (('xf', 0, 128), ('yf', 128, 128), ('zq', 256, 256)), (('xf', 0, 256), ('zq', 256, 256)), (('xf', 0, 256), ('zq', 256, 256)))
REDUCE = ((('xf', 0, 512),), (('yf', 0, 384), ('xf', 384, 128)), (('yf', 0, 384), ('xf', 384, 128)), (('yf', 0, 384), ('xf', 384, 128)))
PLAN = (
    ('start', 0, 0), ('start', 1, 0), ('start', 1, 1), ('start', 1, 2), ('transpose', 0),
    ('relay1', 0, 0), ('relay1', 1, 1), ('relay1', 1, 0), ('transpose', 1), ('relay2', 0, 0),
    ('relay2', 1, 1), ('relay1', 1, 2), ('start', 2, 0), ('relay3', 1, 1), ('start', 2, 1),
    ('relay2', 1, 0), ('relay3', 0, 0), ('start', 3, 0), ('pass1', 0, 0), ('start', 3, 1),
    ('relay2', 1, 2), ('relay1', 2, 0), ('pass2', 0, 0), ('relay1', 2, 1), ('relay3', 1, 2),
    ('pass1', 1, 2), ('relay1', 3, 0), ('forward', 0), ('relay2', 2, 0), ('relay2', 2, 1),
    ('relay1', 3, 1), ('grad', 0, 0), ('relay2', 3, 0), ('pass2', 1, 2), ('grad', 0, 1),
    ('grad', 0, 2), ('relay2', 3, 1), ('grad', 0, 3), ('relay3', 2, 1), ('pass1', 2, 1),
    ('rs_x2', 0, 0), ('forward', 1), ('relay3', 3, 1), ('pass1', 3, 1), ('pass2', 2, 1),
    ('grad', 1, 0), ('grad', 1, 1), ('grad', 1, 2), ('grad', 1, 3), ('x3', 0, 0),
    ('pass2', 3, 1), ('x1a', 1, 0), ('rs_x2', 1, 1), ('forward', 2), ('grad', 2, 0),
    ('grad', 2, 1), ('x1b', 1, 0), ('rs_x2', 1, 0), ('x3', 1, 1), ('rs_z', 0),
    ('grad', 2, 2), ('grad', 2, 3), ('x1a', 2, 0), ('rs_x2', 2, 1), ('forward', 3),
    ('rs_yh', 0), ('rs_z', 1), ('grad', 3, 0), ('grad', 3, 1), ('grad', 3, 2),
    ('x1b', 2, 0), ('back', 0), ('rs_x2', 2, 0), ('x3', 2, 1), ('grad', 3, 3),
    ('rs_yh', 1), ('x1a', 3, 0), ('rs_x2', 3, 1), ('ig_theirs', 0), ('done', 0),
    ('ig_theirs', 1), ('ig_theirs', 2), ('rs_z', 2), ('x1b', 3, 0), ('rs_x2', 3, 0),
    ('ig_theirs', 3), ('back', 1), ('x3', 3, 1), ('ig_mine', 0), ('rs_yh', 2),
    ('ig_mine', 1), ('rs_z', 3), ('ig_mine', 2), ('done', 1), ('back', 2),
    ('ig_mine', 3), ('back', 3), ('done', 2), ('done', 3),
)

WIDTHS = tuple(128 if half else 256 for _, half in CHUNKS)
NCHUNK = len(CHUNKS)
N_IN, N_OUT = 88, 14


def adamw(master, moment_first, moment_second, grad):
    first_next = 0.9 * moment_first + 0.1 * grad
    second_next = 0.95 * moment_second + 0.05 * grad * grad
    corrected_one = first_next / bias_first
    corrected_two = second_next / bias_second
    update = corrected_one / (jnp.sqrt(corrected_two) + 1e-08) + 0.1 * master
    return (master - 0.01 * update, first_next, second_next)


def add(*values):
    total = values[0].astype(f32)
    for v in values[1:]:
        total = total + v.astype(f32)
    return total


def start_col(k):
    return sum(WIDTHS[:k])


def buffers(n, k):
    shapes = [(8, UNIT, n), (HALF, n), (8, UNIT, n), (4, UNIT, n), (2, UNIT, n), (2, 2, UNIT, n)]
    shapes += [(7, 64, n) if FAR[k] else (3, 128, n), (3, 128, n), (2, HALF, n)]
    return [pltpu.VMEM(shape, bf16) for shape in shapes]


N_BUF = 9


def kernel(tokens, hidden, master, ig_out, g_out, tok, tok_t, hid, mst, branch, ig_in, *rest):
    per_chunk = [rest[i * N_BUF : (i + 1) * N_BUF] for i in range(NCHUNK)]
    w, snd, g, yr, x1, x2, zr, yh, fin = zip(*per_chunk)
    lsem, ssem, rsem = rest[NCHUNK * N_BUF :]

    rep, shard = lax.axis_index("rep"), lax.axis_index("shard")
    z, y_hi = rep // 2, rep % 2
    y_lo, x, c = shard // 8, (shard // 2) % 4, shard % 2
    y = y_hi * 2 + y_lo
    mine = y_lo * 4 + x
    across = (1 - y_lo) * 4 + x

    def device(dx=0, dy=0, dz=0, dc=0):
        xx, yy, zz, cc = (x + dx + 4) % 4, (y + dy + 4) % 4, (z + dz + 4) % 4, (c + dc) % 2
        return (zz * 2 + yy // 2, ((yy % 2) * 4 + xx) * 2 + cc)

    sibling = device(dc=1)
    right, left = device(dx=1), device(dx=-1)
    up, down = device(dy=1), device(dy=-1)
    far_y = device(dy=2)
    z_next = [device(dz=1), device(dz=-1), device(dz=2)]
    across_x = device(dx=2)
    group = [(dz, dy) for dy in (2, 0) for dz in (1, -1, 2, 0)]
    partners = [right, left, across_x, up, down] + [device(dz=dz, dy=dy) for dz, dy in group[:7]]
    partners += [device(dz=dz, dy=dy, dc=1) for dz, dy in group]

    def cut_of(size):
        tiles, left_over = divmod(size, 16 * 128 * 2)
        fits = [wide for wide in range(1, 9) if tiles % wide == 0 and tiles // wide <= D // 16]
        return (tiles // fits[-1] * 16, fits[-1] * 128) if fits and not left_over else None

    def some_bytes(size):
        rows, columns = cut_of(size)
        return tok_t.at[pl.ds(0, rows), pl.ds(0, columns)]

    only_apart = []
    outgoing, inboxes = [], []

    def awaiting(size, out, into):
        ref = some_bytes(size)
        return pltpu.make_async_remote_copy(
            src_ref=ref, dst_ref=ref, send_sem=ssem.at[out], recv_sem=rsem.at[into],
            device_id=sibling, device_id_type=MESH,
        )

    class Inbox:
        def __init__(self):
            self.index, self.size, self.waited = len(inboxes), 0, False
            inboxes.append(self)

        def wait_recv(self):
            assert self.size and not self.waited
            self.waited = True
            awaiting(self.size, 0, self.index).wait_recv()

    def send(src, dst, to, into=None):
        into = Inbox() if into is None else into
        size = 2 * math.prod(src.shape)
        if not outgoing or (outgoing[-1] > 3 * 2**20 and cut_of(outgoing[-1])):
            outgoing.append(0)
        outgoing[-1] += size
        into.size += size
        pltpu.make_async_remote_copy(
            src_ref=src, dst_ref=dst, send_sem=ssem.at[len(outgoing) - 1], recv_sem=rsem.at[into.index],
            device_id=to, device_id_type=MESH,
        ).start()
        return into

    local = []

    def fetch(src, dst):
        copy = pltpu.make_async_copy(src, dst, lsem.at[len(local)])
        copy.start()
        local.append(copy)
        return copy

    def hidden_cols(core):
        return pl.ds(pl.multiple_of(core * 384, 128), 512)

    got_master = fetch(master, mst)
    got_tok = fetch(tokens, tok.at[pl.ds(0, TOK)])
    got_hid = fetch(hidden.at[:, hidden_cols(c)], hid.at[pl.ds(0, TOK)])

    barrier = pltpu.get_barrier_semaphore()
    for p in partners:
        pl.semaphore_signal(barrier, inc=1, device_id=p, device_id_type=MESH)
    pl.semaphore_wait(barrier, len(partners))

    my_rows = pl.ds(pl.multiple_of(c * HALF, HALF), HALF)

    def block_of(core, k):
        b = CHUNKS[k][0]
        return 3 if b == 3 else core * 4 + b

    def cols(core, k, part):
        return pl.ds(pl.multiple_of(part * FFW + block_of(core, k) * 128, 128), 128)

    def side(core, k):
        return core if CHUNKS[k][0] == 3 else CHUNKS[k][1] - 1

    def gate_lanes(core, k, shape):
        low = lax.broadcasted_iota(jnp.int32, shape, 1) < 64
        return jnp.logical_xor(low, jnp.broadcast_to(side(core, k) == 1, shape))

    def chunk_of(core, k):
        gate, upw = mst[:, cols(core, k, 0)], mst[:, cols(core, k, 1)]
        if CHUNKS[k][1]:
            return [jnp.where(gate_lanes(core, k, gate.shape), gate, pltpu.roll(upw, 64, 1)).astype(bf16)]
        return [gate.astype(bf16), upw.astype(bf16)]

    got_master.wait()
    swapped = []
    for k in range(NCHUNK):
        for i, (ours, others) in enumerate(zip(chunk_of(c, k), chunk_of(1 - c, k))):
            w[k][mine, my_rows, pl.ds(i * 128, 128)] = ours
            snd[k][:, pl.ds(i * 128, 128)] = others
        swapped.append(send(snd[k], w[k].at[mine, my_rows], sibling))
    tok_in = send(tokens, tok.at[pl.ds(TOK, TOK)], sibling)
    hid_in = send(hidden.at[:, hidden_cols(1 - c)], hid.at[pl.ds(TOK, TOK)], sibling)

    def unit_x(dx):
        return y_lo * 4 + (x + dx + 4) % 4

    gat = {}
    theirs4 = pl.ds((1 - y_lo) * 4, 4)

    def relay(k, unit, rows, to, into):
        part = w[k].at[unit, rows]
        send(part, part, to, into)

    def inbox(*key):
        if key not in gat:
            gat[key] = Inbox()
        return gat[key]

    class Rows:
        def __init__(self, k, m):
            self.mode, base, size = GATHER[k][m]
            self.base, self.size = base, size
            if self.mode == "zq":
                size = size // 4
                base = base + z * size
            step = size // 2
            align = 16
            self.all = pl.ds(pl.multiple_of(base, align), size)
            self.a = pl.ds(pl.multiple_of(base, align), step)
            self.b = pl.ds(pl.multiple_of(base + step, align), step)

        def along_z(self, dz, second):
            step = self.size // 8
            first = self.base + ((z + dz + 4) % 4) * (self.size // 4) + second * step
            return pl.ds(pl.multiple_of(first, 16), step)

    part_of = {(k, m): Rows(k, m) for k in range(NCHUNK) for m in range(len(GATHER[k]))}

    def to_y(k, m, name, unit):
        r = part_of[k, m]
        relay(k, unit, r.a, up, inbox(k, m, name))
        relay(k, unit, r.b, down, inbox(k, m, name))

    def to_z(k, m, name, unit):
        r = part_of[k, m]
        for there in z_next[:2]:
            relay(k, unit, r.all, there, inbox(k, m, name))

    def on_z(k, m, unit):
        r = part_of[k, m]
        relay(k, unit, r.along_z(-1, 0), z_next[0], inbox(k, m, "zf"))
        relay(k, unit, r.along_z(1, 1), z_next[1], inbox(k, m, "zf"))

    def landed(*key):
        gat[key].wait_recv()

    def both_x(k, m, name, unit):
        r = part_of[k, m]
        for there in (right, left):
            relay(k, unit, r.all, there, inbox(k, m, name))

    def on_x(k, m, name, row):
        r = part_of[k, m]
        landed(k, m, name)
        relay(k, row * 4 + (x + 3) % 4, r.a, right, inbox(k, m, "xf"))
        relay(k, row * 4 + (x + 1) % 4, r.b, left, inbox(k, m, "xf"))

    def start(k, m):
        if m == 0:
            swapped[k].wait_recv()
        if part_of[k, m].mode == "xd":
            relay(k, mine, part_of[k, m].all, across_x, inbox(k, m, "xf"))
        if part_of[k, m].mode == "yf":
            to_y(k, m, "y", mine)
            both_x(k, m, "x", mine)
        else:
            both_x(k, m, "x", mine)
            to_y(k, m, "y", mine)

    def relay1(k, m):
        mode = part_of[k, m].mode
        if mode == "yf":
            landed(k, m, "y")
            both_x(k, m, "o", across)
            return
        if mode == "xd":
            landed(k, m, "x")
        else:
            on_x(k, m, "x", y_lo)
        for dx in (-1, 1):
            to_y(k, m, "y", unit_x(dx))
            if mode == "zq":
                to_z(k, m, "z", unit_x(dx))

    def relay2(k, m):
        mode = part_of[k, m].mode
        if mode == "yf":
            on_x(k, m, "x", y_lo)
            return
        landed(k, m, "xf")
        to_y(k, m, "y", unit_x(2))
        if mode == "zq":
            to_z(k, m, "z", unit_x(2))

    def relay3(k, m):
        if part_of[k, m].mode == "yf":
            on_x(k, m, "o", 1 - y_lo)
            return
        landed(k, m, "y")
        to_z(k, m, "z4", theirs4)

    def pass1(k, m):
        landed(k, m, "z")
        for dx in (-1, 1, 2):
            on_z(k, m, unit_x(dx))

    def pass2(k, m):
        landed(k, m, "z4")
        on_z(k, m, theirs4)

    def gathered(k):
        for m in range(len(GATHER[k])):
            landed(k, m, {"yf": "xf", "xf": "y", "xd": "y", "zq": "zf"}[part_of[k, m].mode])

    def transpose(half):
        (got_tok.wait, tok_in.wait_recv)[half]()

        @pl.loop(0, 8)
        def _(i):
            cut = pl.ds(pl.multiple_of(i * 512, 512), 512)
            tok_t[cut, pl.ds(half * TOK, TOK)] = tok[pl.ds(half * TOK, TOK), cut].T

        if half == 1:
            got_hid.wait()
            hid_in.wait_recv()

    def forward(k):
        gathered(k)
        n, here = WIDTHS[k], start_col(k)
        block = CHUNKS[k][0]
        at = (1 - c) * 384 if block == 3 else (c + block) * 128

        @pl.loop(0, 2)
        def _(i):
            rows = pl.ds(pl.multiple_of(i * 512, 512), 512)
            gu = jnp.dot(tok[rows, :], w[k][...].reshape(D, n), preferred_element_type=f32) * MULT
            h = hid[rows, pl.ds(pl.multiple_of(at, 128), 128)].astype(f32)
            half = CHUNKS[k][1]
            gate, upw = (gu, pltpu.roll(gu, 64, 1)) if half else (gu[:, :128], gu[:, 128:])
            s = jax.nn.sigmoid(gate)
            d_gate = h * upw * s * (1.0 + gate * (1.0 - s))
            d_up = h * gate * s
            if half:
                mixed = jnp.where(gate_lanes(c, k, gu.shape), d_gate, pltpu.roll(d_up, 64, 1))
                branch[rows, pl.ds(here, 128)] = mixed.astype(bf16)
            else:
                branch[rows, pl.ds(here, 128)] = d_gate.astype(bf16)
                branch[rows, pl.ds(here + 128, 128)] = d_up.astype(bf16)

    red = {}

    def in_turn(j):
        return (x + 2 + j) % 4

    def halves(base, size):
        return pl.ds(base, size // 2), pl.ds(base + size // 2, size // 2)

    def grad(k, j):
        n = WIDTHS[k]

        @pl.loop(0, 2)
        def _(i):
            unit = ((i + 1 - y_lo) % 2) * 4 + in_turn(j)
            rows = pl.ds(pl.multiple_of(unit * UNIT, UNIT), UNIT)
            got = jnp.dot(tok_t[rows, :], branch[:, pl.ds(start_col(k), n)], preferred_element_type=f32)
            g[k][unit] = (got * MULT).astype(bf16)

        for m, (mode, base, size) in enumerate(REDUCE[k]):
            a, b = halves(base, size)
            if mode in ("yf", "yd"):
                unit, box = (1 - y_lo) * 4 + in_turn(j), Inbox()
                send(g[k].at[unit, a], yr[k].at[in_turn(j), a], up, box)
                send(g[k].at[unit, b], yr[k].at[in_turn(j), b], down, box)
                red[k, m, "y", j] = box
            elif j == 0:
                red[k, m, "x1"] = box = Inbox()
                for u in range(2):
                    send(g[k].at[u * 4 + in_turn(0), a], x1[k].at[u, a], right, box)
                    send(g[k].at[u * 4 + in_turn(0), b], x1[k].at[u, b], left, box)

    def plus(k, unit, rows, *others):
        g[k][unit, rows, :] = add(g[k][unit, rows, :], *others).astype(bf16)

    def take_y(k, m, j):
        _, base, size = REDUCE[k][m]
        red[k, m, "y", j].wait_recv()
        rows = pl.ds(base, size)
        plus(k, y_lo * 4 + in_turn(j), rows, yr[k][in_turn(j), rows, :])

    def x1a(k, m):
        mode, base, size = REDUCE[k][m]
        rows, (a, b) = pl.ds(base, size), halves(base, size)
        take_y(k, m, 0)
        if mode == "yd":
            red[k, m, "x2"] = send(g[k].at[unit_x(2), rows], x2[k].at[0, 1, rows], across_x)
            return
        red[k, m, "x1"] = box = Inbox()
        send(g[k].at[unit_x(2), a], x1[k].at[0, a], right, box)
        send(g[k].at[unit_x(2), b], x1[k].at[0, b], left, box)

    def x1b(k, m):
        mode, base, size = REDUCE[k][m]
        rows = pl.ds(base, size)
        for j in (1, 3, 2):
            take_y(k, m, j)
            if mode == "yd" and j != 2:
                there, slot = ((left, 1), None, (right, 0))[j - 1]
                send(g[k].at[y_lo * 4 + in_turn(j), rows], x2[k].at[slot, 0, rows], there, red[k, m, "x2"])

    def rs_x2(k, m):
        mode, base, size = REDUCE[k][m]
        rows, (a, b) = pl.ds(base, size), halves(base, size)
        if mode == "yd":
            return
        red[k, m, "x1"].wait_recv()
        red[k, m, "x2"] = box = Inbox()
        for u, row in ((0, y_lo),) if mode == "yf" else ((0, 0), (1, 1)):
            here = row * 4 + (x + 1) % 4
            plus(k, here, a, x1[k][u, a, :])
            send(g[k].at[here, rows], x2[k].at[0, u, rows], right, box)
            here = row * 4 + (x + 3) % 4
            plus(k, here, b, x1[k][u, b, :])
            send(g[k].at[here, rows], x2[k].at[1, u, rows], left, box)

    def x3(k, m):
        _, base, size = REDUCE[k][m]
        rows, (a, b) = pl.ds(base, size), halves(base, size)
        red[k, m, "x2"].wait_recv()
        for u in range(2):
            plus(k, u * 4 + x, rows, x2[k][0, u, rows, :], x2[k][1, u, rows, :])
        red[k, m, "y"] = box = Inbox()
        send(g[k].at[across, a], yr[k].at[0, a], up, box)
        send(g[k].at[across, b], yr[k].at[0, b], down, box)

    def quarter(dz):
        return pl.ds(pl.multiple_of(((z + dz + 4) % 4) * 128, 128), 128)

    def share(dz, dy):
        return pl.ds(pl.multiple_of((((z + dz + 4) % 4) * 2 + (y_hi + dy // 2) % 2) * 64, 64), 64)

    def rs_z(k):
        for m, (mode, base, size) in enumerate(REDUCE[k]):
            rows = pl.ds(base, size)
            if mode == "xf":
                red[k, m, "y"].wait_recv()
                plus(k, mine, rows, yr[k][0, rows, :])
                continue
            red[k, m, "x2"].wait_recv()
            third = [x2[k][0, 1, rows, :]] if mode == "yd" else []
            plus(k, mine, rows, x2[k][0, 0, rows, :], x2[k][1, 0, rows, :], *third)
        red[k, "z"] = box = Inbox()
        if FAR[k]:
            for j, (dz, dy) in enumerate(group[:7]):
                send(g[k].at[mine, share(dz, dy)], zr[k].at[j], device(dz=dz, dy=dy), box)
            return
        for j, dz in enumerate((1, -1, 2)):
            send(g[k].at[mine, quarter(dz)], zr[k].at[j], z_next[j], box)

    def rs_yh(k):
        if FAR[k]:
            return
        red[k, "z"].wait_recv()
        total = add(g[k][mine, quarter(0), :], zr[k][0], zr[k][1], zr[k][2])
        yh[k][0] = total.astype(bf16)
        red[k, "yh"] = send(yh[k].at[0], yh[k].at[1], far_y)

    def back(k):
        owner, rows = z // 2, 64 if FAR[k] else 128
        if FAR[k]:
            red[k, "z"].wait_recv()
            total = add(g[k][mine, share(0, 0), :], *(zr[k][j] for j in range(7)))
            first = (z % 2) * 128 + y_hi * 64
        else:
            red[k, "yh"].wait_recv()
            total = add(yh[k][0], yh[k][1])
            first = (z % 2) * 128
        part = yh[k].at[2, pl.ds(0, rows)]
        part[...] = total.astype(bf16)
        there = fin[k].at[c, pl.ds(pl.multiple_of(first, 64), rows)]
        red[k, "back"] = box = Inbox()
        for dz, dy in group[:7] if FAR[k] else group[4:7]:
            zz, yy = (z + dz + 4) % 4, (y + dy) % 4
            send(part, there, (zz * 2 + yy // 2, (y_lo * 4 + x) * 2 + owner), box)
        size = 2 * rows * WIDTHS[k]
        box.size += size
        outgoing.append(size)
        alone = len(outgoing) - 1
        only_apart.append(alone)

        @pl.when(c != owner)
        def _():
            pltpu.make_async_remote_copy(
                src_ref=part, dst_ref=there, send_sem=ssem.at[alone], recv_sem=rsem.at[box.index],
                device_id=sibling, device_id_type=MESH,
            ).start()

        @pl.when(c == owner)
        def _():
            pltpu.make_async_copy(part, there, rsem.at[box.index]).start()

        outgoing.append(0)

    def done(k):
        red[k, "back"].wait_recv()
        own, theirs = fin[k][c], fin[k][1 - c]
        block, half = CHUNKS[k]
        if not half:
            for core, value in ((c, own), (1 - c, theirs)):
                g_out[:, cols(core, k, 0)] = value[:, :128]
                g_out[:, cols(core, k, 1)] = value[:, 128:]
            return
        gates = gate_lanes(c, k, own.shape)
        if block == 3:
            g_out[:, cols(c, k, 0)] = jnp.where(gates, own, theirs)
            g_out[:, cols(c, k, 1)] = pltpu.roll(jnp.where(gates, theirs, own).astype(f32), 64, 1).astype(bf16)
            return
        for core, value in ((c, own), (1 - c, theirs)):
            for part, lanes in ((0, value), (1, pltpu.roll(value.astype(f32), 64, 1).astype(bf16))):
                if half == 2:
                    lanes = jnp.where(gates, lanes, g_out[:, cols(core, k, part)])
                g_out[:, cols(core, k, part)] = lanes

    ig = {}

    def ig_dot(rows, unit):
        total = None
        for k in range(NCHUNK):
            part = lax.dot_general(
                branch[rows, pl.ds(start_col(k), WIDTHS[k])], w[k][unit],
                (((1,), (1,)), ((), ())), preferred_element_type=f32,
            )
            total = part if total is None else total + part
        return total * MULT

    def group_cols(j):
        return pl.ds(j * 1024, 1024)

    def ig_theirs(j):
        @pl.loop(0, 2)
        def _(i):
            unit = j * 2 + i
            cut = pl.ds(pl.multiple_of(unit * 512, 512), 512)
            tok[pl.ds(0, TOK), cut] = ig_dot(pl.ds(TOK, TOK), unit).astype(bf16)

        ig[j] = send(tok.at[pl.ds(0, TOK), group_cols(j)], ig_in.at[:, group_cols(j)], sibling)

    def ig_mine(j):
        ig[j].wait_recv()

        @pl.loop(0, 2)
        def _(i):
            unit = j * 2 + i
            cut = pl.ds(pl.multiple_of(unit * 512, 512), 512)
            value = ig_dot(pl.ds(0, TOK), unit) + ig_in[:, cut].astype(f32)
            tok[pl.ds(TOK, TOK), cut] = value.astype(bf16)

        ig[j, "out"] = fetch(tok.at[pl.ds(TOK, TOK), group_cols(j)], ig_out.at[:, group_cols(j)])

    steps = dict(
        start=start, relay1=relay1, relay2=relay2, relay3=relay3, pass1=pass1, pass2=pass2, transpose=transpose,
        forward=forward, grad=grad, x1a=x1a, x1b=x1b, rs_x2=rs_x2, x3=x3, rs_z=rs_z, rs_yh=rs_yh, back=back,
        done=done, ig_theirs=ig_theirs, ig_mine=ig_mine,
    )
    for name, *which in PLAN:
        steps[name](*which)
    for j in range(4):
        ig[j, "out"].wait()
    assert all(box.waited for box in inboxes) and len(inboxes) <= N_IN and len(outgoing) <= N_OUT
    for i, size in enumerate(outgoing):
        if i in only_apart:

            @pl.when(c != z // 2)
            def _():
                awaiting(size, i, 0).wait_send()

        elif size:
            awaiting(size, i, 0).wait_send()


def fused(tokens, hidden, master):
    anywhere = pl.BlockSpec(memory_space=pl.ANY)
    vmem = pl.BlockSpec(memory_space=pltpu.VMEM)
    return pl.pallas_call(
        kernel,
        out_shape=[jax.ShapeDtypeStruct((TOK, D), bf16), jax.ShapeDtypeStruct((HALF, 2 * FFW), bf16)],
        in_specs=[anywhere] * 3,
        out_specs=[anywhere, vmem],
        scratch_shapes=[
            pltpu.VMEM((2 * TOK, D), bf16),
            pltpu.VMEM((D, 2 * TOK), bf16),
            pltpu.VMEM((2 * TOK, 512), bf16),
            pltpu.VMEM((HALF, 2 * FFW), f32),
            pltpu.VMEM((2 * TOK, FFW), bf16),
            pltpu.VMEM((TOK, D), bf16),
            *(ref for k in range(NCHUNK) for ref in buffers(WIDTHS[k], k)),
            pltpu.SemaphoreType.DMA((8,)),
            pltpu.SemaphoreType.DMA((N_OUT,)),
            pltpu.SemaphoreType.DMA((N_IN,)),
        ],
        compiler_params=pltpu.CompilerParams(
            collective_id=0, has_side_effects=True, vmem_limit_bytes=63 * 2**20
        ),
        cost_estimate=pl.CostEstimate(flops=22_500_000_000, bytes_accessed=20_000_000, transcendentals=1_000_000),
    )(tokens, hidden, master)


def body(tokens, hidden_grad, master, moment_first, moment_second):
    input_grad, grad = fused(tokens, hidden_grad, master)
    master_next, first_next, second_next = adamw(master, moment_first, moment_second, grad.astype(f32))
    return (input_grad, master_next, first_next, second_next)


def solution(mesh):
    return jax.shard_map(
        body,
        mesh=mesh,
        in_specs=(
            P(("rep", "shard"), None),
            P(("rep", "shard"), None),
            P("shard", None),
            P("shard", None),
            P("shard", None),
        ),
        out_specs=(P(("rep", "shard"), None), P("shard", None), P("shard", None), P("shard", None)),
        check_vma=False,
    )
```

```python
import math

import jax
import jax.numpy as jnp
from jax import lax
from jax.experimental import pallas as pl
from jax.experimental.pallas import tpu as pltpu
from jax.sharding import PartitionSpec as P

MESH = pl.DeviceIdType.MESH
bias_first = 0.999973438601
bias_second = 0.99407947078
bf16, f32 = jnp.bfloat16, jnp.float32

D, FFW, TOK = 4096, 896, 512
UNIT = 512
HALF = 256
MULT = 1.0 / 64.0
CHUNKS = ((3, 1), (0, 0), (1, 0), (2, 0))
FAR = (False, False, False, True)
GATHER = ((('zq', 0, 512),), (('xf', 0, 128), ('yf', 128, 128), ('zq', 256, 256)), (('xf', 0, 256), ('yf', 256, 256)), (('zq', 0, 512),))
REDUCE = ((('yf', 0, 256), ('xf', 256, 256)), (('yf', 0, 384), ('xf', 384, 128)), (('yf', 0, 384), ('xf', 384, 128)), (('yf', 0, 384), ('xf', 384, 128)))
PLAN = (
    ('start', 0, 0), ('start', 1, 0), ('start', 1, 1), ('start', 1, 2), ('transpose', 0),
    ('relay1', 0, 0), ('relay1', 1, 1), ('relay1', 1, 0), ('transpose', 1), ('relay2', 0, 0),
    ('relay2', 1, 1), ('relay1', 1, 2), ('start', 2, 0), ('relay3', 1, 1), ('start', 2, 1),
    ('relay2', 1, 0), ('relay3', 0, 0), ('pass1', 0, 0), ('relay2', 1, 2), ('relay1', 2, 0),
    ('relay1', 2, 1), ('start', 3, 0), ('pass2', 0, 0), ('relay3', 1, 2), ('pass1', 1, 2),
    ('relay2', 2, 1), ('forward', 0), ('relay2', 2, 0), ('grad', 0, 0), ('pass2', 1, 2),
    ('grad', 0, 1), ('relay3', 2, 1), ('grad', 0, 2), ('relay1', 3, 0), ('grad', 0, 3),
    ('x1a', 0, 0), ('forward', 1), ('rs_x2', 0, 1), ('x1b', 0, 0), ('relay2', 3, 0),
    ('grad', 1, 0), ('rs_x2', 0, 0), ('grad', 1, 1), ('relay3', 3, 0), ('grad', 1, 2),
    ('pass1', 3, 0), ('x3', 0, 1), ('grad', 1, 3), ('x1a', 1, 0), ('rs_x2', 1, 1),
    ('forward', 2), ('grad', 2, 0), ('rs_z', 0), ('pass2', 3, 0), ('grad', 2, 1),
    ('grad', 2, 2), ('x1b', 1, 0), ('rs_x2', 1, 0), ('x3', 1, 1), ('rs_yh', 0),
    ('x1a', 2, 0), ('grad', 2, 3), ('rs_x2', 2, 1), ('forward', 3), ('grad', 3, 0),
    ('back', 0), ('rs_z', 1), ('grad', 3, 1), ('x1b', 2, 0), ('rs_x2', 2, 0),
    ('grad', 3, 2), ('done', 0), ('x1a', 3, 0), ('x3', 2, 1), ('grad', 3, 3),
    ('rs_x2', 3, 1), ('ig_theirs', 0), ('rs_yh', 1), ('ig_theirs', 1), ('ig_theirs', 2),
    ('rs_z', 2), ('x1b', 3, 0), ('rs_x2', 3, 0), ('back', 1), ('ig_theirs', 3),
    ('x3', 3, 1), ('ig_mine', 0), ('rs_yh', 2), ('ig_mine', 1), ('rs_z', 3),
    ('done', 1), ('ig_mine', 2), ('back', 2), ('ig_mine', 3), ('back', 3),
    ('done', 2), ('done', 3),
)

WIDTHS = tuple(128 if half else 256 for _, half in CHUNKS)
NCHUNK = len(CHUNKS)
N_IN, N_OUT = 89, 14


def adamw(master, moment_first, moment_second, grad):
    first_next = 0.9 * moment_first + 0.1 * grad
    second_next = 0.95 * moment_second + 0.05 * grad * grad
    corrected_one = first_next / bias_first
    corrected_two = second_next / bias_second
    update = corrected_one / (jnp.sqrt(corrected_two) + 1e-08) + 0.1 * master
    return (master - 0.01 * update, first_next, second_next)


def add(*values):
    total = values[0].astype(f32)
    for v in values[1:]:
        total = total + v.astype(f32)
    return total


def start_col(k):
    return sum(WIDTHS[:k])


def buffers(n, k):
    shapes = [(8, UNIT, n), (HALF, n), (8, UNIT, n), (4, UNIT, n), (2, UNIT, n), (2, 2, UNIT, n)]
    shapes += [(7, 64, n) if FAR[k] else (3, 128, n), (3, 128, n), (2, HALF, n)]
    return [pltpu.VMEM(shape, bf16) for shape in shapes]


N_BUF = 9


def kernel(tokens, hidden, master, ig_out, g_out, tok, tok_t, hid, mst, branch, ig_in, *rest):
    per_chunk = [rest[i * N_BUF : (i + 1) * N_BUF] for i in range(NCHUNK)]
    w, snd, g, yr, x1, x2, zr, yh, fin = zip(*per_chunk)
    lsem, ssem, rsem = rest[NCHUNK * N_BUF :]

    rep, shard = lax.axis_index("rep"), lax.axis_index("shard")
    z, y_hi = rep // 2, rep % 2
    y_lo, x, c = shard // 8, (shard // 2) % 4, shard % 2
    y = y_hi * 2 + y_lo
    mine = y_lo * 4 + x
    across = (1 - y_lo) * 4 + x

    def device(dx=0, dy=0, dz=0, dc=0):
        xx, yy, zz, cc = (x + dx + 4) % 4, (y + dy + 4) % 4, (z + dz + 4) % 4, (c + dc) % 2
        return (zz * 2 + yy // 2, ((yy % 2) * 4 + xx) * 2 + cc)

    sibling = device(dc=1)
    right, left = device(dx=1), device(dx=-1)
    up, down = device(dy=1), device(dy=-1)
    far_y = device(dy=2)
    z_next = [device(dz=1), device(dz=-1), device(dz=2)]
    across_x = device(dx=2)
    group = [(dz, dy) for dy in (2, 0) for dz in (1, -1, 2, 0)]
    partners = [right, left, across_x, up, down] + [device(dz=dz, dy=dy) for dz, dy in group[:7]]
    partners += [device(dz=dz, dy=dy, dc=1) for dz, dy in group]

    def cut_of(size):
        tiles, left_over = divmod(size, 16 * 128 * 2)
        fits = [wide for wide in range(1, 9) if tiles % wide == 0 and tiles // wide <= D // 16]
        return (tiles // fits[-1] * 16, fits[-1] * 128) if fits and not left_over else None

    def some_bytes(size):
        rows, columns = cut_of(size)
        return tok_t.at[pl.ds(0, rows), pl.ds(0, columns)]

    only_apart = []
    outgoing, inboxes = [], []

    def awaiting(size, out, into):
        ref = some_bytes(size)
        return pltpu.make_async_remote_copy(
            src_ref=ref, dst_ref=ref, send_sem=ssem.at[out], recv_sem=rsem.at[into],
            device_id=sibling, device_id_type=MESH,
        )

    class Inbox:
        def __init__(self):
            self.index, self.size, self.waited = len(inboxes), 0, False
            inboxes.append(self)

        def wait_recv(self):
            assert self.size and not self.waited
            self.waited = True
            awaiting(self.size, 0, self.index).wait_recv()

    def send(src, dst, to, into=None):
        into = Inbox() if into is None else into
        size = 2 * math.prod(src.shape)
        if not outgoing or (outgoing[-1] > 3 * 2**20 and cut_of(outgoing[-1])):
            outgoing.append(0)
        outgoing[-1] += size
        into.size += size
        pltpu.make_async_remote_copy(
            src_ref=src, dst_ref=dst, send_sem=ssem.at[len(outgoing) - 1], recv_sem=rsem.at[into.index],
            device_id=to, device_id_type=MESH,
        ).start()
        return into

    local = []

    def fetch(src, dst):
        copy = pltpu.make_async_copy(src, dst, lsem.at[len(local)])
        copy.start()
        local.append(copy)
        return copy

    def hidden_cols(core):
        return pl.ds(pl.multiple_of(core * 384, 128), 512)

    got_master = fetch(master, mst)
    got_tok = fetch(tokens, tok.at[pl.ds(0, TOK)])
    got_hid = fetch(hidden.at[:, hidden_cols(c)], hid.at[pl.ds(0, TOK)])

    barrier = pltpu.get_barrier_semaphore()
    for p in partners:
        pl.semaphore_signal(barrier, inc=1, device_id=p, device_id_type=MESH)
    pl.semaphore_wait(barrier, len(partners))

    my_rows = pl.ds(pl.multiple_of(c * HALF, HALF), HALF)

    def block_of(core, k):
        b = CHUNKS[k][0]
        return 3 if b == 3 else core * 4 + b

    def cols(core, k, part):
        return pl.ds(pl.multiple_of(part * FFW + block_of(core, k) * 128, 128), 128)

    def side(core, k):
        return core if CHUNKS[k][0] == 3 else CHUNKS[k][1] - 1

    def gate_lanes(core, k, shape):
        low = lax.broadcasted_iota(jnp.int32, shape, 1) < 64
        return jnp.logical_xor(low, jnp.broadcast_to(side(core, k) == 1, shape))

    def chunk_of(core, k):
        gate, upw = mst[:, cols(core, k, 0)], mst[:, cols(core, k, 1)]
        if CHUNKS[k][1]:
            return [jnp.where(gate_lanes(core, k, gate.shape), gate, pltpu.roll(upw, 64, 1)).astype(bf16)]
        return [gate.astype(bf16), upw.astype(bf16)]

    got_master.wait()
    swapped = []
    for k in range(NCHUNK):
        for i, (ours, others) in enumerate(zip(chunk_of(c, k), chunk_of(1 - c, k))):
            w[k][mine, my_rows, pl.ds(i * 128, 128)] = ours
            snd[k][:, pl.ds(i * 128, 128)] = others
        swapped.append(send(snd[k], w[k].at[mine, my_rows], sibling))
    tok_in = send(tokens, tok.at[pl.ds(TOK, TOK)], sibling)
    hid_in = send(hidden.at[:, hidden_cols(1 - c)], hid.at[pl.ds(TOK, TOK)], sibling)

    def unit_x(dx):
        return y_lo * 4 + (x + dx + 4) % 4

    gat = {}
    theirs4 = pl.ds((1 - y_lo) * 4, 4)

    def relay(k, unit, rows, to, into):
        part = w[k].at[unit, rows]
        send(part, part, to, into)

    def inbox(*key):
        if key not in gat:
            gat[key] = Inbox()
        return gat[key]

    class Rows:
        def __init__(self, k, m):
            self.mode, base, size = GATHER[k][m]
            self.base, self.size = base, size
            if self.mode == "zq":
                size = size // 4
                base = base + z * size
            step = size // 2
            align = 16
            self.all = pl.ds(pl.multiple_of(base, align), size)
            self.a = pl.ds(pl.multiple_of(base, align), step)
            self.b = pl.ds(pl.multiple_of(base + step, align), step)

        def along_z(self, dz, second):
            step = self.size // 8
            first = self.base + ((z + dz + 4) % 4) * (self.size // 4) + second * step
            return pl.ds(pl.multiple_of(first, 16), step)

    part_of = {(k, m): Rows(k, m) for k in range(NCHUNK) for m in range(len(GATHER[k]))}

    def to_y(k, m, name, unit):
        r = part_of[k, m]
        relay(k, unit, r.a, up, inbox(k, m, name))
        relay(k, unit, r.b, down, inbox(k, m, name))

    def to_z(k, m, name, unit):
        r = part_of[k, m]
        for there in z_next[:2]:
            relay(k, unit, r.all, there, inbox(k, m, name))

    def on_z(k, m, unit):
        r = part_of[k, m]
        relay(k, unit, r.along_z(-1, 0), z_next[0], inbox(k, m, "zf"))
        relay(k, unit, r.along_z(1, 1), z_next[1], inbox(k, m, "zf"))

    def landed(*key):
        gat[key].wait_recv()

    def both_x(k, m, name, unit):
        r = part_of[k, m]
        for there in (right, left):
            relay(k, unit, r.all, there, inbox(k, m, name))

    def on_x(k, m, name, row):
        r = part_of[k, m]
        landed(k, m, name)
        relay(k, row * 4 + (x + 3) % 4, r.a, right, inbox(k, m, "xf"))
        relay(k, row * 4 + (x + 1) % 4, r.b, left, inbox(k, m, "xf"))

    def start(k, m):
        if m == 0:
            swapped[k].wait_recv()
        if part_of[k, m].mode == "xd":
            relay(k, mine, part_of[k, m].all, across_x, inbox(k, m, "xf"))
        if part_of[k, m].mode == "yf":
            to_y(k, m, "y", mine)
            both_x(k, m, "x", mine)
        else:
            both_x(k, m, "x", mine)
            to_y(k, m, "y", mine)

    def relay1(k, m):
        mode = part_of[k, m].mode
        if mode == "yf":
            landed(k, m, "y")
            both_x(k, m, "o", across)
            return
        if mode == "xd":
            landed(k, m, "x")
        else:
            on_x(k, m, "x", y_lo)
        for dx in (-1, 1):
            to_y(k, m, "y", unit_x(dx))
            if mode == "zq":
                to_z(k, m, "z", unit_x(dx))

    def relay2(k, m):
        mode = part_of[k, m].mode
        if mode == "yf":
            on_x(k, m, "x", y_lo)
            return
        landed(k, m, "xf")
        to_y(k, m, "y", unit_x(2))
        if mode == "zq":
            to_z(k, m, "z", unit_x(2))

    def relay3(k, m):
        if part_of[k, m].mode == "yf":
            on_x(k, m, "o", 1 - y_lo)
            return
        landed(k, m, "y")
        to_z(k, m, "z4", theirs4)

    def pass1(k, m):
        landed(k, m, "z")
        for dx in (-1, 1, 2):
            on_z(k, m, unit_x(dx))

    def pass2(k, m):
        landed(k, m, "z4")
        on_z(k, m, theirs4)

    def gathered(k):
        for m in range(len(GATHER[k])):
            landed(k, m, {"yf": "xf", "xf": "y", "xd": "y", "zq": "zf"}[part_of[k, m].mode])

    def transpose(half):
        (got_tok.wait, tok_in.wait_recv)[half]()

        @pl.loop(0, 8)
        def _(i):
            cut = pl.ds(pl.multiple_of(i * 512, 512), 512)
            tok_t[cut, pl.ds(half * TOK, TOK)] = tok[pl.ds(half * TOK, TOK), cut].T

        if half == 1:
            got_hid.wait()
            hid_in.wait_recv()

    def forward(k):
        gathered(k)
        n, here = WIDTHS[k], start_col(k)
        block = CHUNKS[k][0]
        at = (1 - c) * 384 if block == 3 else (c + block) * 128

        @pl.loop(0, 2)
        def _(i):
            rows = pl.ds(pl.multiple_of(i * 512, 512), 512)
            gu = jnp.dot(tok[rows, :], w[k][...].reshape(D, n), preferred_element_type=f32) * MULT
            h = hid[rows, pl.ds(pl.multiple_of(at, 128), 128)].astype(f32)
            half = CHUNKS[k][1]
            gate, upw = (gu, pltpu.roll(gu, 64, 1)) if half else (gu[:, :128], gu[:, 128:])
            s = jax.nn.sigmoid(gate)
            d_gate = h * upw * s * (1.0 + gate * (1.0 - s))
            d_up = h * gate * s
            if half:
                mixed = jnp.where(gate_lanes(c, k, gu.shape), d_gate, pltpu.roll(d_up, 64, 1))
                branch[rows, pl.ds(here, 128)] = mixed.astype(bf16)
            else:
                branch[rows, pl.ds(here, 128)] = d_gate.astype(bf16)
                branch[rows, pl.ds(here + 128, 128)] = d_up.astype(bf16)

    red = {}

    def in_turn(j):
        return (x + 2 + j) % 4

    def halves(base, size):
        return pl.ds(base, size // 2), pl.ds(base + size // 2, size // 2)

    def grad(k, j):
        n = WIDTHS[k]

        @pl.loop(0, 2)
        def _(i):
            unit = ((i + 1 - y_lo) % 2) * 4 + in_turn(j)
            rows = pl.ds(pl.multiple_of(unit * UNIT, UNIT), UNIT)
            got = jnp.dot(tok_t[rows, :], branch[:, pl.ds(start_col(k), n)], preferred_element_type=f32)
            g[k][unit] = (got * MULT).astype(bf16)

        for m, (mode, base, size) in enumerate(REDUCE[k]):
            a, b = halves(base, size)
            if mode in ("yf", "yd"):
                unit, box = (1 - y_lo) * 4 + in_turn(j), Inbox()
                send(g[k].at[unit, a], yr[k].at[in_turn(j), a], up, box)
                send(g[k].at[unit, b], yr[k].at[in_turn(j), b], down, box)
                red[k, m, "y", j] = box
            elif j == 0:
                red[k, m, "x1"] = box = Inbox()
                for u in range(2):
                    send(g[k].at[u * 4 + in_turn(0), a], x1[k].at[u, a], right, box)
                    send(g[k].at[u * 4 + in_turn(0), b], x1[k].at[u, b], left, box)

    def plus(k, unit, rows, *others):
        g[k][unit, rows, :] = add(g[k][unit, rows, :], *others).astype(bf16)

    def take_y(k, m, j):
        _, base, size = REDUCE[k][m]
        red[k, m, "y", j].wait_recv()
        rows = pl.ds(base, size)
        plus(k, y_lo * 4 + in_turn(j), rows, yr[k][in_turn(j), rows, :])

    def x1a(k, m):
        mode, base, size = REDUCE[k][m]
        rows, (a, b) = pl.ds(base, size), halves(base, size)
        take_y(k, m, 0)
        if mode == "yd":
            red[k, m, "x2"] = send(g[k].at[unit_x(2), rows], x2[k].at[0, 1, rows], across_x)
            return
        red[k, m, "x1"] = box = Inbox()
        send(g[k].at[unit_x(2), a], x1[k].at[0, a], right, box)
        send(g[k].at[unit_x(2), b], x1[k].at[0, b], left, box)

    def x1b(k, m):
        mode, base, size = REDUCE[k][m]
        rows = pl.ds(base, size)
        for j in (1, 3, 2):
            take_y(k, m, j)
            if mode == "yd" and j != 2:
                there, slot = ((left, 1), None, (right, 0))[j - 1]
                send(g[k].at[y_lo * 4 + in_turn(j), rows], x2[k].at[slot, 0, rows], there, red[k, m, "x2"])

    def rs_x2(k, m):
        mode, base, size = REDUCE[k][m]
        rows, (a, b) = pl.ds(base, size), halves(base, size)
        if mode == "yd":
            return
        red[k, m, "x1"].wait_recv()
        red[k, m, "x2"] = box = Inbox()
        for u, row in ((0, y_lo),) if mode == "yf" else ((0, 0), (1, 1)):
            here = row * 4 + (x + 1) % 4
            plus(k, here, a, x1[k][u, a, :])
            send(g[k].at[here, rows], x2[k].at[0, u, rows], right, box)
            here = row * 4 + (x + 3) % 4
            plus(k, here, b, x1[k][u, b, :])
            send(g[k].at[here, rows], x2[k].at[1, u, rows], left, box)

    def x3(k, m):
        _, base, size = REDUCE[k][m]
        rows, (a, b) = pl.ds(base, size), halves(base, size)
        red[k, m, "x2"].wait_recv()
        for u in range(2):
            plus(k, u * 4 + x, rows, x2[k][0, u, rows, :], x2[k][1, u, rows, :])
        red[k, m, "y"] = box = Inbox()
        send(g[k].at[across, a], yr[k].at[0, a], up, box)
        send(g[k].at[across, b], yr[k].at[0, b], down, box)

    def quarter(dz):
        return pl.ds(pl.multiple_of(((z + dz + 4) % 4) * 128, 128), 128)

    def share(dz, dy):
        return pl.ds(pl.multiple_of((((z + dz + 4) % 4) * 2 + (y_hi + dy // 2) % 2) * 64, 64), 64)

    def rs_z(k):
        for m, (mode, base, size) in enumerate(REDUCE[k]):
            rows = pl.ds(base, size)
            if mode == "xf":
                red[k, m, "y"].wait_recv()
                plus(k, mine, rows, yr[k][0, rows, :])
                continue
            red[k, m, "x2"].wait_recv()
            third = [x2[k][0, 1, rows, :]] if mode == "yd" else []
            plus(k, mine, rows, x2[k][0, 0, rows, :], x2[k][1, 0, rows, :], *third)
        red[k, "z"] = box = Inbox()
        if FAR[k]:
            for j, (dz, dy) in enumerate(group[:7]):
                send(g[k].at[mine, share(dz, dy)], zr[k].at[j], device(dz=dz, dy=dy), box)
            return
        for j, dz in enumerate((1, -1, 2)):
            send(g[k].at[mine, quarter(dz)], zr[k].at[j], z_next[j], box)

    def rs_yh(k):
        if FAR[k]:
            return
        red[k, "z"].wait_recv()
        total = add(g[k][mine, quarter(0), :], zr[k][0], zr[k][1], zr[k][2])
        yh[k][0] = total.astype(bf16)
        red[k, "yh"] = send(yh[k].at[0], yh[k].at[1], far_y)

    def back(k):
        owner, rows = z // 2, 64 if FAR[k] else 128
        if FAR[k]:
            red[k, "z"].wait_recv()
            total = add(g[k][mine, share(0, 0), :], *(zr[k][j] for j in range(7)))
            first = (z % 2) * 128 + y_hi * 64
        else:
            red[k, "yh"].wait_recv()
            total = add(yh[k][0], yh[k][1])
            first = (z % 2) * 128
        part = yh[k].at[2, pl.ds(0, rows)]
        part[...] = total.astype(bf16)
        there = fin[k].at[c, pl.ds(pl.multiple_of(first, 64), rows)]
        red[k, "back"] = box = Inbox()
        for dz, dy in group[:7] if FAR[k] else group[4:7]:
            zz, yy = (z + dz + 4) % 4, (y + dy) % 4
            send(part, there, (zz * 2 + yy // 2, (y_lo * 4 + x) * 2 + owner), box)
        size = 2 * rows * WIDTHS[k]
        box.size += size
        outgoing.append(size)
        alone = len(outgoing) - 1
        only_apart.append(alone)

        @pl.when(c != owner)
        def _():
            pltpu.make_async_remote_copy(
                src_ref=part, dst_ref=there, send_sem=ssem.at[alone], recv_sem=rsem.at[box.index],
                device_id=sibling, device_id_type=MESH,
            ).start()

        @pl.when(c == owner)
        def _():
            pltpu.make_async_copy(part, there, rsem.at[box.index]).start()

        outgoing.append(0)

    def done(k):
        red[k, "back"].wait_recv()
        own, theirs = fin[k][c], fin[k][1 - c]
        block, half = CHUNKS[k]
        if not half:
            for core, value in ((c, own), (1 - c, theirs)):
                g_out[:, cols(core, k, 0)] = value[:, :128]
                g_out[:, cols(core, k, 1)] = value[:, 128:]
            return
        gates = gate_lanes(c, k, own.shape)
        if block == 3:
            g_out[:, cols(c, k, 0)] = jnp.where(gates, own, theirs)
            g_out[:, cols(c, k, 1)] = pltpu.roll(jnp.where(gates, theirs, own).astype(f32), 64, 1).astype(bf16)
            return
        for core, value in ((c, own), (1 - c, theirs)):
            for part, lanes in ((0, value), (1, pltpu.roll(value.astype(f32), 64, 1).astype(bf16))):
                if half == 2:
                    lanes = jnp.where(gates, lanes, g_out[:, cols(core, k, part)])
                g_out[:, cols(core, k, part)] = lanes

    ig = {}

    def ig_dot(rows, unit):
        total = None
        for k in range(NCHUNK):
            part = lax.dot_general(
                branch[rows, pl.ds(start_col(k), WIDTHS[k])], w[k][unit],
                (((1,), (1,)), ((), ())), preferred_element_type=f32,
            )
            total = part if total is None else total + part
        return total * MULT

    def group_cols(j):
        return pl.ds(j * 1024, 1024)

    def ig_theirs(j):
        @pl.loop(0, 2)
        def _(i):
            unit = j * 2 + i
            cut = pl.ds(pl.multiple_of(unit * 512, 512), 512)
            tok[pl.ds(0, TOK), cut] = ig_dot(pl.ds(TOK, TOK), unit).astype(bf16)

        ig[j] = send(tok.at[pl.ds(0, TOK), group_cols(j)], ig_in.at[:, group_cols(j)], sibling)

    def ig_mine(j):
        ig[j].wait_recv()

        @pl.loop(0, 2)
        def _(i):
            unit = j * 2 + i
            cut = pl.ds(pl.multiple_of(unit * 512, 512), 512)
            value = ig_dot(pl.ds(0, TOK), unit) + ig_in[:, cut].astype(f32)
            tok[pl.ds(TOK, TOK), cut] = value.astype(bf16)

        ig[j, "out"] = fetch(tok.at[pl.ds(TOK, TOK), group_cols(j)], ig_out.at[:, group_cols(j)])

    steps = dict(
        start=start, relay1=relay1, relay2=relay2, relay3=relay3, pass1=pass1, pass2=pass2, transpose=transpose,
        forward=forward, grad=grad, x1a=x1a, x1b=x1b, rs_x2=rs_x2, x3=x3, rs_z=rs_z, rs_yh=rs_yh, back=back,
        done=done, ig_theirs=ig_theirs, ig_mine=ig_mine,
    )
    for name, *which in PLAN:
        steps[name](*which)
    for j in range(4):
        ig[j, "out"].wait()
    assert all(box.waited for box in inboxes) and len(inboxes) <= N_IN and len(outgoing) <= N_OUT
    for i, size in enumerate(outgoing):
        if i in only_apart:

            @pl.when(c != z // 2)
            def _():
                awaiting(size, i, 0).wait_send()

        elif size:
            awaiting(size, i, 0).wait_send()


def fused(tokens, hidden, master):
    anywhere = pl.BlockSpec(memory_space=pl.ANY)
    vmem = pl.BlockSpec(memory_space=pltpu.VMEM)
    return pl.pallas_call(
        kernel,
        out_shape=[jax.ShapeDtypeStruct((TOK, D), bf16), jax.ShapeDtypeStruct((HALF, 2 * FFW), bf16)],
        in_specs=[anywhere] * 3,
        out_specs=[anywhere, vmem],
        scratch_shapes=[
            pltpu.VMEM((2 * TOK, D), bf16),
            pltpu.VMEM((D, 2 * TOK), bf16),
            pltpu.VMEM((2 * TOK, 512), bf16),
            pltpu.VMEM((HALF, 2 * FFW), f32),
            pltpu.VMEM((2 * TOK, FFW), bf16),
            pltpu.VMEM((TOK, D), bf16),
            *(ref for k in range(NCHUNK) for ref in buffers(WIDTHS[k], k)),
            pltpu.SemaphoreType.DMA((8,)),
            pltpu.SemaphoreType.DMA((N_OUT,)),
            pltpu.SemaphoreType.DMA((N_IN,)),
        ],
        compiler_params=pltpu.CompilerParams(
            collective_id=0, has_side_effects=True, vmem_limit_bytes=63 * 2**20
        ),
        cost_estimate=pl.CostEstimate(flops=22_500_000_000, bytes_accessed=20_000_000, transcendentals=1_000_000),
    )(tokens, hidden, master)


def body(tokens, hidden_grad, master, moment_first, moment_second):
    input_grad, grad = fused(tokens, hidden_grad, master)
    master_next, first_next, second_next = adamw(master, moment_first, moment_second, grad.astype(f32))
    return (input_grad, master_next, first_next, second_next)


def solution(mesh):
    return jax.shard_map(
        body,
        mesh=mesh,
        in_specs=(
            P(("rep", "shard"), None),
            P(("rep", "shard"), None),
            P("shard", None),
            P("shard", None),
            P("shard", None),
        ),
        out_specs=(P(("rep", "shard"), None), P("shard", None), P("shard", None), P("shard", None)),
        check_vma=False,
    )
```

```python
import math

import jax
import jax.numpy as jnp
from jax import lax
from jax.experimental import pallas as pl
from jax.experimental.pallas import tpu as pltpu
from jax.sharding import PartitionSpec as P

MESH = pl.DeviceIdType.MESH
bias_first = 0.999973438601
bias_second = 0.99407947078
bf16, f32 = jnp.bfloat16, jnp.float32

D, FFW, TOK = 4096, 896, 512
UNIT = 512
HALF = 256
MULT = 1.0 / 64.0
CHUNKS = ((3, 1), (0, 0), (1, 0), (2, 0))
FAR = (False, False, False, True)
GATHER = ((('zq', 0, 512),), (('xf', 0, 128), ('yf', 128, 128), ('zq', 256, 256)), (('xf', 0, 256), ('yf', 256, 256)), (('zq', 0, 512),))
REDUCE = ((('yf', 0, 256), ('xf', 256, 256)), (('yf', 0, 384), ('xf', 384, 128)), (('yf', 0, 384), ('xf', 384, 128)), (('yf', 0, 384), ('xf', 384, 128)))
PLAN = (
    ('start', 0, 0), ('start', 1, 0), ('start', 1, 1), ('start', 1, 2), ('transpose', 0),
    ('relay1', 0, 0), ('relay1', 1, 1), ('relay1', 1, 0), ('transpose', 1), ('relay2', 0, 0),
    ('relay2', 1, 1), ('relay1', 1, 2), ('start', 2, 0), ('relay3', 1, 1), ('start', 2, 1),
    ('relay2', 1, 0), ('relay3', 0, 0), ('pass1', 0, 0), ('relay2', 1, 2), ('relay1', 2, 0),
    ('relay1', 2, 1), ('start', 3, 0), ('pass2', 0, 0), ('relay3', 1, 2), ('pass1', 1, 2),
    ('relay2', 2, 1), ('forward', 0), ('relay2', 2, 0), ('grad', 0, 0), ('pass2', 1, 2),
    ('grad', 0, 1), ('relay3', 2, 1), ('grad', 0, 2), ('relay1', 3, 0), ('grad', 0, 3),
    ('x1a', 0, 0), ('forward', 1), ('rs_x2', 0, 1), ('x1b', 0, 0), ('relay2', 3, 0),
    ('grad', 1, 0), ('rs_x2', 0, 0), ('grad', 1, 1), ('relay3', 3, 0), ('grad', 1, 2),
    ('pass1', 3, 0), ('x3', 0, 1), ('grad', 1, 3), ('x1a', 1, 0), ('rs_x2', 1, 1),
    ('forward', 2), ('grad', 2, 0), ('rs_z', 0), ('pass2', 3, 0), ('grad', 2, 1),
    ('grad', 2, 2), ('x1b', 1, 0), ('rs_x2', 1, 0), ('x3', 1, 1), ('rs_yh', 0),
    ('x1a', 2, 0), ('grad', 2, 3), ('rs_x2', 2, 1), ('forward', 3), ('grad', 3, 0),
    ('back', 0), ('rs_z', 1), ('grad', 3, 1), ('x1b', 2, 0), ('rs_x2', 2, 0),
    ('grad', 3, 2), ('done', 0), ('x1a', 3, 0), ('x3', 2, 1), ('grad', 3, 3),
    ('rs_x2', 3, 1), ('ig_theirs', 0), ('rs_yh', 1), ('ig_theirs', 1), ('ig_theirs', 2),
    ('rs_z', 2), ('x1b', 3, 0), ('rs_x2', 3, 0), ('back', 1), ('ig_theirs', 3),
    ('x3', 3, 1), ('ig_mine', 0), ('rs_yh', 2), ('ig_mine', 1), ('rs_z', 3),
    ('done', 1), ('ig_mine', 2), ('back', 2), ('ig_mine', 3), ('back', 3),
    ('done', 2), ('done', 3),
)

WIDTHS = tuple(128 if half else 256 for _, half in CHUNKS)
NCHUNK = len(CHUNKS)
N_IN, N_OUT = 89, 14


def adamw(master, moment_first, moment_second, grad):
    first_next = 0.9 * moment_first + 0.1 * grad
    second_next = 0.95 * moment_second + 0.05 * grad * grad
    corrected_one = first_next / bias_first
    corrected_two = second_next / bias_second
    update = corrected_one / (jnp.sqrt(corrected_two) + 1e-08) + 0.1 * master
    return (master - 0.01 * update, first_next, second_next)


def add(*values):
    total = values[0].astype(f32)
    for v in values[1:]:
        total = total + v.astype(f32)
    return total


def start_col(k):
    return sum(WIDTHS[:k])


def buffers(n, k):
    shapes = [(8, UNIT, n), (HALF, n), (8, UNIT, n), (4, UNIT, n), (2, UNIT, n), (2, 2, UNIT, n)]
    shapes += [(7, 64, n) if FAR[k] else (3, 128, n), (3, 128, n), (2, HALF, n)]
    return [pltpu.VMEM(shape, bf16) for shape in shapes]


N_BUF = 9


def kernel(tokens, hidden, master, ig_out, g_out, tok, tok_t, hid, mst, branch, ig_in, *rest):
    per_chunk = [rest[i * N_BUF : (i + 1) * N_BUF] for i in range(NCHUNK)]
    w, snd, g, yr, x1, x2, zr, yh, fin = zip(*per_chunk)
    lsem, ssem, rsem = rest[NCHUNK * N_BUF :]

    rep, shard = lax.axis_index("rep"), lax.axis_index("shard")
    z, y_hi = rep // 2, rep % 2
    y_lo, x, c = shard // 8, (shard // 2) % 4, shard % 2
    y = y_hi * 2 + y_lo
    mine = y_lo * 4 + x
    across = (1 - y_lo) * 4 + x

    def device(dx=0, dy=0, dz=0, dc=0):
        xx, yy, zz, cc = (x + dx + 4) % 4, (y + dy + 4) % 4, (z + dz + 4) % 4, (c + dc) % 2
        return (zz * 2 + yy // 2, ((yy % 2) * 4 + xx) * 2 + cc)

    sibling = device(dc=1)
    right, left = device(dx=1), device(dx=-1)
    up, down = device(dy=1), device(dy=-1)
    far_y = device(dy=2)
    z_next = [device(dz=1), device(dz=-1), device(dz=2)]
    across_x = device(dx=2)
    group = [(dz, dy) for dy in (2, 0) for dz in (1, -1, 2, 0)]
    partners = [right, left, across_x, up, down] + [device(dz=dz, dy=dy) for dz, dy in group[:7]]
    partners += [device(dz=dz, dy=dy, dc=1) for dz, dy in group]

    def cut_of(size):
        tiles, left_over = divmod(size, 16 * 128 * 2)
        fits = [wide for wide in range(1, 9) if tiles % wide == 0 and tiles // wide <= D // 16]
        return (tiles // fits[-1] * 16, fits[-1] * 128) if fits and not left_over else None

    def some_bytes(size):
        rows, columns = cut_of(size)
        return tok_t.at[pl.ds(0, rows), pl.ds(0, columns)]

    only_apart = []
    outgoing, inboxes = [], []

    def awaiting(size, out, into):
        ref = some_bytes(size)
        return pltpu.make_async_remote_copy(
            src_ref=ref, dst_ref=ref, send_sem=ssem.at[out], recv_sem=rsem.at[into],
            device_id=sibling, device_id_type=MESH,
        )

    class Inbox:
        def __init__(self):
            self.index, self.size, self.waited = len(inboxes), 0, False
            inboxes.append(self)

        def wait_recv(self):
            assert self.size and not self.waited
            self.waited = True
            awaiting(self.size, 0, self.index).wait_recv()

    def send(src, dst, to, into=None):
        into = Inbox() if into is None else into
        size = 2 * math.prod(src.shape)
        if not outgoing or (outgoing[-1] > 3 * 2**20 and cut_of(outgoing[-1])):
            outgoing.append(0)
        outgoing[-1] += size
        into.size += size
        pltpu.make_async_remote_copy(
            src_ref=src, dst_ref=dst, send_sem=ssem.at[len(outgoing) - 1], recv_sem=rsem.at[into.index],
            device_id=to, device_id_type=MESH,
        ).start()
        return into

    local = []

    def fetch(src, dst):
        copy = pltpu.make_async_copy(src, dst, lsem.at[len(local)])
        copy.start()
        local.append(copy)
        return copy

    def hidden_cols(core):
        return pl.ds(pl.multiple_of(core * 384, 128), 512)

    got_master = fetch(master, mst)
    got_tok = fetch(tokens, tok.at[pl.ds(0, TOK)])
    got_hid = fetch(hidden.at[:, hidden_cols(c)], hid.at[pl.ds(0, TOK)])

    barrier = pltpu.get_barrier_semaphore()
    for p in partners:
        pl.semaphore_signal(barrier, inc=1, device_id=p, device_id_type=MESH)
    pl.semaphore_wait(barrier, len(partners))

    my_rows = pl.ds(pl.multiple_of(c * HALF, HALF), HALF)

    def block_of(core, k):
        b = CHUNKS[k][0]
        return 3 if b == 3 else core * 4 + b

    def cols(core, k, part):
        return pl.ds(pl.multiple_of(part * FFW + block_of(core, k) * 128, 128), 128)

    def side(core, k):
        return core if CHUNKS[k][0] == 3 else CHUNKS[k][1] - 1

    def gate_lanes(core, k, shape):
        low = lax.broadcasted_iota(jnp.int32, shape, 1) < 64
        return jnp.logical_xor(low, jnp.broadcast_to(side(core, k) == 1, shape))

    def chunk_of(core, k):
        gate, upw = mst[:, cols(core, k, 0)], mst[:, cols(core, k, 1)]
        if CHUNKS[k][1]:
            return [jnp.where(gate_lanes(core, k, gate.shape), gate, pltpu.roll(upw, 64, 1)).astype(bf16)]
        return [gate.astype(bf16), upw.astype(bf16)]

    got_master.wait()
    swapped = []
    for k in range(NCHUNK):
        for i, (ours, others) in enumerate(zip(chunk_of(c, k), chunk_of(1 - c, k))):
            w[k][mine, my_rows, pl.ds(i * 128, 128)] = ours
            snd[k][:, pl.ds(i * 128, 128)] = others
        swapped.append(send(snd[k], w[k].at[mine, my_rows], sibling))
    tok_in = send(tokens, tok.at[pl.ds(TOK, TOK)], sibling)
    hid_in = send(hidden.at[:, hidden_cols(1 - c)], hid.at[pl.ds(TOK, TOK)], sibling)

    def unit_x(dx):
        return y_lo * 4 + (x + dx + 4) % 4

    gat = {}
    theirs4 = pl.ds((1 - y_lo) * 4, 4)

    def relay(k, unit, rows, to, into):
        part = w[k].at[unit, rows]
        send(part, part, to, into)

    def inbox(*key):
        if key not in gat:
            gat[key] = Inbox()
        return gat[key]

    class Rows:
        def __init__(self, k, m):
            self.mode, base, size = GATHER[k][m]
            self.base, self.size = base, size
            if self.mode == "zq":
                size = size // 4
                base = base + z * size
            step = size // 2
            align = 16
            self.all = pl.ds(pl.multiple_of(base, align), size)
            self.a = pl.ds(pl.multiple_of(base, align), step)
            self.b = pl.ds(pl.multiple_of(base + step, align), step)

        def along_z(self, dz, second):
            step = self.size // 8
            first = self.base + ((z + dz + 4) % 4) * (self.size // 4) + second * step
            return pl.ds(pl.multiple_of(first, 16), step)

    part_of = {(k, m): Rows(k, m) for k in range(NCHUNK) for m in range(len(GATHER[k]))}

    def to_y(k, m, name, unit):
        r = part_of[k, m]
        relay(k, unit, r.a, up, inbox(k, m, name))
        relay(k, unit, r.b, down, inbox(k, m, name))

    def to_z(k, m, name, unit):
        r = part_of[k, m]
        for there in z_next[:2]:
            relay(k, unit, r.all, there, inbox(k, m, name))

    def on_z(k, m, unit):
        r = part_of[k, m]
        relay(k, unit, r.along_z(-1, 0), z_next[0], inbox(k, m, "zf"))
        relay(k, unit, r.along_z(1, 1), z_next[1], inbox(k, m, "zf"))

    def landed(*key):
        gat[key].wait_recv()

    def both_x(k, m, name, unit):
        r = part_of[k, m]
        for there in (right, left):
            relay(k, unit, r.all, there, inbox(k, m, name))

    def on_x(k, m, name, row):
        r = part_of[k, m]
        landed(k, m, name)
        relay(k, row * 4 + (x + 3) % 4, r.a, right, inbox(k, m, "xf"))
        relay(k, row * 4 + (x + 1) % 4, r.b, left, inbox(k, m, "xf"))

    def start(k, m):
        if m == 0:
            swapped[k].wait_recv()
        if part_of[k, m].mode == "xd":
            relay(k, mine, part_of[k, m].all, across_x, inbox(k, m, "xf"))
        if part_of[k, m].mode == "yf":
            to_y(k, m, "y", mine)
            both_x(k, m, "x", mine)
        else:
            both_x(k, m, "x", mine)
            to_y(k, m, "y", mine)

    def relay1(k, m):
        mode = part_of[k, m].mode
        if mode == "yf":
            landed(k, m, "y")
            both_x(k, m, "o", across)
            return
        if mode == "xd":
            landed(k, m, "x")
        else:
            on_x(k, m, "x", y_lo)
        for dx in (-1, 1):
            to_y(k, m, "y", unit_x(dx))
            if mode == "zq":
                to_z(k, m, "z", unit_x(dx))

    def relay2(k, m):
        mode = part_of[k, m].mode
        if mode == "yf":
            on_x(k, m, "x", y_lo)
            return
        landed(k, m, "xf")
        to_y(k, m, "y", unit_x(2))
        if mode == "zq":
            to_z(k, m, "z", unit_x(2))

    def relay3(k, m):
        if part_of[k, m].mode == "yf":
            on_x(k, m, "o", 1 - y_lo)
            return
        landed(k, m, "y")
        to_z(k, m, "z4", theirs4)

    def pass1(k, m):
        landed(k, m, "z")
        for dx in (-1, 1, 2):
            on_z(k, m, unit_x(dx))

    def pass2(k, m):
        landed(k, m, "z4")
        on_z(k, m, theirs4)

    def gathered(k):
        for m in range(len(GATHER[k])):
            landed(k, m, {"yf": "xf", "xf": "y", "xd": "y", "zq": "zf"}[part_of[k, m].mode])

    def transpose(half):
        (got_tok.wait, tok_in.wait_recv)[half]()

        @pl.loop(0, 8)
        def _(i):
            cut = pl.ds(pl.multiple_of(i * 512, 512), 512)
            tok_t[cut, pl.ds(half * TOK, TOK)] = tok[pl.ds(half * TOK, TOK), cut].T

        if half == 1:
            got_hid.wait()
            hid_in.wait_recv()

    def forward(k):
        gathered(k)
        n, here = WIDTHS[k], start_col(k)
        block = CHUNKS[k][0]
        at = (1 - c) * 384 if block == 3 else (c + block) * 128

        @pl.loop(0, 2, unroll=True)
        def _(i):
            rows = pl.ds(pl.multiple_of(i * 512, 512), 512)
            gu = jnp.dot(tok[rows, :], w[k][...].reshape(D, n), preferred_element_type=f32) * MULT
            h = hid[rows, pl.ds(pl.multiple_of(at, 128), 128)].astype(f32)
            half = CHUNKS[k][1]
            gate, upw = (gu, pltpu.roll(gu, 64, 1)) if half else (gu[:, :128], gu[:, 128:])
            s = jax.nn.sigmoid(gate)
            d_gate = h * upw * s * (1.0 + gate * (1.0 - s))
            d_up = h * gate * s
            if half:
                mixed = jnp.where(gate_lanes(c, k, gu.shape), d_gate, pltpu.roll(d_up, 64, 1))
                branch[rows, pl.ds(here, 128)] = mixed.astype(bf16)
            else:
                branch[rows, pl.ds(here, 128)] = d_gate.astype(bf16)
                branch[rows, pl.ds(here + 128, 128)] = d_up.astype(bf16)

    red = {}

    def in_turn(j):
        return (x + 2 + j) % 4

    def halves(base, size):
        return pl.ds(base, size // 2), pl.ds(base + size // 2, size // 2)

    def grad(k, j):
        n = WIDTHS[k]

        @pl.loop(0, 2)
        def _(i):
            unit = ((i + 1 - y_lo) % 2) * 4 + in_turn(j)
            rows = pl.ds(pl.multiple_of(unit * UNIT, UNIT), UNIT)
            got = jnp.dot(tok_t[rows, :], branch[:, pl.ds(start_col(k), n)], preferred_element_type=f32)
            g[k][unit] = (got * MULT).astype(bf16)

        for m, (mode, base, size) in enumerate(REDUCE[k]):
            a, b = halves(base, size)
            if mode in ("yf", "yd"):
                unit, box = (1 - y_lo) * 4 + in_turn(j), Inbox()
                send(g[k].at[unit, a], yr[k].at[in_turn(j), a], up, box)
                send(g[k].at[unit, b], yr[k].at[in_turn(j), b], down, box)
                red[k, m, "y", j] = box
            elif j == 0:
                red[k, m, "x1"] = box = Inbox()
                for u in range(2):
                    send(g[k].at[u * 4 + in_turn(0), a], x1[k].at[u, a], right, box)
                    send(g[k].at[u * 4 + in_turn(0), b], x1[k].at[u, b], left, box)

    def plus(k, unit, rows, *others):
        g[k][unit, rows, :] = add(g[k][unit, rows, :], *others).astype(bf16)

    def take_y(k, m, j):
        _, base, size = REDUCE[k][m]
        red[k, m, "y", j].wait_recv()
        rows = pl.ds(base, size)
        plus(k, y_lo * 4 + in_turn(j), rows, yr[k][in_turn(j), rows, :])

    def x1a(k, m):
        mode, base, size = REDUCE[k][m]
        rows, (a, b) = pl.ds(base, size), halves(base, size)
        take_y(k, m, 0)
        if mode == "yd":
            red[k, m, "x2"] = send(g[k].at[unit_x(2), rows], x2[k].at[0, 1, rows], across_x)
            return
        red[k, m, "x1"] = box = Inbox()
        send(g[k].at[unit_x(2), a], x1[k].at[0, a], right, box)
        send(g[k].at[unit_x(2), b], x1[k].at[0, b], left, box)

    def x1b(k, m):
        mode, base, size = REDUCE[k][m]
        rows = pl.ds(base, size)
        for j in (1, 3, 2):
            take_y(k, m, j)
            if mode == "yd" and j != 2:
                there, slot = ((left, 1), None, (right, 0))[j - 1]
                send(g[k].at[y_lo * 4 + in_turn(j), rows], x2[k].at[slot, 0, rows], there, red[k, m, "x2"])

    def rs_x2(k, m):
        mode, base, size = REDUCE[k][m]
        rows, (a, b) = pl.ds(base, size), halves(base, size)
        if mode == "yd":
            return
        red[k, m, "x1"].wait_recv()
        red[k, m, "x2"] = box = Inbox()
        for u, row in ((0, y_lo),) if mode == "yf" else ((0, 0), (1, 1)):
            here = row * 4 + (x + 1) % 4
            plus(k, here, a, x1[k][u, a, :])
            send(g[k].at[here, rows], x2[k].at[0, u, rows], right, box)
            here = row * 4 + (x + 3) % 4
            plus(k, here, b, x1[k][u, b, :])
            send(g[k].at[here, rows], x2[k].at[1, u, rows], left, box)

    def x3(k, m):
        _, base, size = REDUCE[k][m]
        rows, (a, b) = pl.ds(base, size), halves(base, size)
        red[k, m, "x2"].wait_recv()
        for u in range(2):
            plus(k, u * 4 + x, rows, x2[k][0, u, rows, :], x2[k][1, u, rows, :])
        red[k, m, "y"] = box = Inbox()
        send(g[k].at[across, a], yr[k].at[0, a], up, box)
        send(g[k].at[across, b], yr[k].at[0, b], down, box)

    def quarter(dz):
        return pl.ds(pl.multiple_of(((z + dz + 4) % 4) * 128, 128), 128)

    def share(dz, dy):
        return pl.ds(pl.multiple_of((((z + dz + 4) % 4) * 2 + (y_hi + dy // 2) % 2) * 64, 64), 64)

    def rs_z(k):
        for m, (mode, base, size) in enumerate(REDUCE[k]):
            rows = pl.ds(base, size)
            if mode == "xf":
                red[k, m, "y"].wait_recv()
                plus(k, mine, rows, yr[k][0, rows, :])
                continue
            red[k, m, "x2"].wait_recv()
            third = [x2[k][0, 1, rows, :]] if mode == "yd" else []
            plus(k, mine, rows, x2[k][0, 0, rows, :], x2[k][1, 0, rows, :], *third)
        red[k, "z"] = box = Inbox()
        if FAR[k]:
            for j, (dz, dy) in enumerate(group[:7]):
                send(g[k].at[mine, share(dz, dy)], zr[k].at[j], device(dz=dz, dy=dy), box)
            return
        for j, dz in enumerate((1, -1, 2)):
            send(g[k].at[mine, quarter(dz)], zr[k].at[j], z_next[j], box)

    def rs_yh(k):
        if FAR[k]:
            return
        red[k, "z"].wait_recv()
        total = add(g[k][mine, quarter(0), :], zr[k][0], zr[k][1], zr[k][2])
        yh[k][0] = total.astype(bf16)
        red[k, "yh"] = send(yh[k].at[0], yh[k].at[1], far_y)

    def back(k):
        owner, rows = z // 2, 64 if FAR[k] else 128
        if FAR[k]:
            red[k, "z"].wait_recv()
            total = add(g[k][mine, share(0, 0), :], *(zr[k][j] for j in range(7)))
            first = (z % 2) * 128 + y_hi * 64
        else:
            red[k, "yh"].wait_recv()
            total = add(yh[k][0], yh[k][1])
            first = (z % 2) * 128
        part = yh[k].at[2, pl.ds(0, rows)]
        part[...] = total.astype(bf16)
        there = fin[k].at[c, pl.ds(pl.multiple_of(first, 64), rows)]
        red[k, "back"] = box = Inbox()
        for dz, dy in group[:7] if FAR[k] else group[4:7]:
            zz, yy = (z + dz + 4) % 4, (y + dy) % 4
            send(part, there, (zz * 2 + yy // 2, (y_lo * 4 + x) * 2 + owner), box)
        size = 2 * rows * WIDTHS[k]
        box.size += size
        outgoing.append(size)
        alone = len(outgoing) - 1
        only_apart.append(alone)

        @pl.when(c != owner)
        def _():
            pltpu.make_async_remote_copy(
                src_ref=part, dst_ref=there, send_sem=ssem.at[alone], recv_sem=rsem.at[box.index],
                device_id=sibling, device_id_type=MESH,
            ).start()

        @pl.when(c == owner)
        def _():
            pltpu.make_async_copy(part, there, rsem.at[box.index]).start()

        outgoing.append(0)

    def done(k):
        red[k, "back"].wait_recv()
        own, theirs = fin[k][c], fin[k][1 - c]
        block, half = CHUNKS[k]
        if not half:
            for core, value in ((c, own), (1 - c, theirs)):
                g_out[:, cols(core, k, 0)] = value[:, :128]
                g_out[:, cols(core, k, 1)] = value[:, 128:]
            return
        gates = gate_lanes(c, k, own.shape)
        if block == 3:
            g_out[:, cols(c, k, 0)] = jnp.where(gates, own, theirs)
            g_out[:, cols(c, k, 1)] = pltpu.roll(jnp.where(gates, theirs, own).astype(f32), 64, 1).astype(bf16)
            return
        for core, value in ((c, own), (1 - c, theirs)):
            for part, lanes in ((0, value), (1, pltpu.roll(value.astype(f32), 64, 1).astype(bf16))):
                if half == 2:
                    lanes = jnp.where(gates, lanes, g_out[:, cols(core, k, part)])
                g_out[:, cols(core, k, part)] = lanes

    ig = {}

    def ig_dot(rows, unit):
        total = None
        for k in range(NCHUNK):
            part = lax.dot_general(
                branch[rows, pl.ds(start_col(k), WIDTHS[k])], w[k][unit],
                (((1,), (1,)), ((), ())), preferred_element_type=f32,
            )
            total = part if total is None else total + part
        return total * MULT

    def group_cols(j):
        return pl.ds(j * 1024, 1024)

    def ig_theirs(j):
        @pl.loop(0, 2)
        def _(i):
            unit = j * 2 + i
            cut = pl.ds(pl.multiple_of(unit * 512, 512), 512)
            tok[pl.ds(0, TOK), cut] = ig_dot(pl.ds(TOK, TOK), unit).astype(bf16)

        ig[j] = send(tok.at[pl.ds(0, TOK), group_cols(j)], ig_in.at[:, group_cols(j)], sibling)

    def ig_mine(j):
        ig[j].wait_recv()

        @pl.loop(0, 2)
        def _(i):
            unit = j * 2 + i
            cut = pl.ds(pl.multiple_of(unit * 512, 512), 512)
            value = ig_dot(pl.ds(0, TOK), unit) + ig_in[:, cut].astype(f32)
            tok[pl.ds(TOK, TOK), cut] = value.astype(bf16)

        ig[j, "out"] = fetch(tok.at[pl.ds(TOK, TOK), group_cols(j)], ig_out.at[:, group_cols(j)])

    steps = dict(
        start=start, relay1=relay1, relay2=relay2, relay3=relay3, pass1=pass1, pass2=pass2, transpose=transpose,
        forward=forward, grad=grad, x1a=x1a, x1b=x1b, rs_x2=rs_x2, x3=x3, rs_z=rs_z, rs_yh=rs_yh, back=back,
        done=done, ig_theirs=ig_theirs, ig_mine=ig_mine,
    )
    for name, *which in PLAN:
        steps[name](*which)
    for j in range(4):
        ig[j, "out"].wait()
    assert all(box.waited for box in inboxes) and len(inboxes) <= N_IN and len(outgoing) <= N_OUT
    for i, size in enumerate(outgoing):
        if i in only_apart:

            @pl.when(c != z // 2)
            def _():
                awaiting(size, i, 0).wait_send()

        elif size:
            awaiting(size, i, 0).wait_send()


def fused(tokens, hidden, master):
    anywhere = pl.BlockSpec(memory_space=pl.ANY)
    vmem = pl.BlockSpec(memory_space=pltpu.VMEM)
    return pl.pallas_call(
        kernel,
        out_shape=[jax.ShapeDtypeStruct((TOK, D), bf16), jax.ShapeDtypeStruct((HALF, 2 * FFW), bf16)],
        in_specs=[anywhere] * 3,
        out_specs=[anywhere, vmem],
        scratch_shapes=[
            pltpu.VMEM((2 * TOK, D), bf16),
            pltpu.VMEM((D, 2 * TOK), bf16),
            pltpu.VMEM((2 * TOK, 512), bf16),
            pltpu.VMEM((HALF, 2 * FFW), f32),
            pltpu.VMEM((2 * TOK, FFW), bf16),
            pltpu.VMEM((TOK, D), bf16),
            *(ref for k in range(NCHUNK) for ref in buffers(WIDTHS[k], k)),
            pltpu.SemaphoreType.DMA((8,)),
            pltpu.SemaphoreType.DMA((N_OUT,)),
            pltpu.SemaphoreType.DMA((N_IN,)),
        ],
        compiler_params=pltpu.CompilerParams(
            collective_id=0, has_side_effects=True, vmem_limit_bytes=63 * 2**20
        ),
        cost_estimate=pl.CostEstimate(flops=22_500_000_000, bytes_accessed=20_000_000, transcendentals=1_000_000),
    )(tokens, hidden, master)


def body(tokens, hidden_grad, master, moment_first, moment_second):
    input_grad, grad = fused(tokens, hidden_grad, master)
    master_next, first_next, second_next = adamw(master, moment_first, moment_second, grad.astype(f32))
    return (input_grad, master_next, first_next, second_next)


def solution(mesh):
    return jax.shard_map(
        body,
        mesh=mesh,
        in_specs=(
            P(("rep", "shard"), None),
            P(("rep", "shard"), None),
            P("shard", None),
            P("shard", None),
            P("shard", None),
        ),
        out_specs=(P(("rep", "shard"), None), P("shard", None), P("shard", None), P("shard", None)),
        check_vma=False,
    )
```
